32 devices in a mesh: leaf: 8 (over z, y), sub: 4 (over x, core).
Axes of the slice: x: 2, y: 2, z: 4, core: 2. Of those that a mesh axis runs over, the one named last changes fastest.
Arguments:
- start_vec: float32 [128, 256], P(('leaf', 'sub')), as said below
- near_blocks: bfloat16 [128, 2, 256, 256], P(('leaf', 'sub')), may hold values from -0.25 to 0.25
- near_ids: int32 [128, 1], P(('leaf', 'sub')), may hold values from 0 to 47
- far_ids: int32 [128, 2], P(('leaf', 'sub')), may hold values from 0 to 15
- leaf_basis: bfloat16 [128, 64, 256], P(('leaf', 'sub')), may hold values from -0.375 to 0.375
- leaf_coupling: bfloat16 [128, 64, 128], P(('leaf', 'sub')), may hold values from -0.5 to 0.5
- node_transfer: bfloat16 [32, 64, 256], P(('leaf', 'sub')), may hold values from -0.375 to 0.375
- branch_transfer: bfloat16 [32, 64, 64], P(('leaf', 'sub')), may hold values from -0.75 to 0.75
- top_ids: int32 [8, 4], P('leaf'), may hold values from 0 to 7
- top_coupling: bfloat16 [8, 64, 256], P('leaf'), may hold values from -0.375 to 0.375
Outputs:
- basis: float32 [4, 128, 256], P(None, ('leaf', 'sub'))
- hessen: float32 [4, 3], replicated
The draws below stay inside these ranges and needn't reach their ends.
Inputs may be any that keep to these rules, and one draw needn't show every extreme that they name: start_vec is real-valued with entries of order one.
All inputs are finite; a program needn't handle non-finite values.
Results may differ from the reference program's by a relative error of at most 0.02.
Values may be sent and summed in bfloat16 or wider, within the bound.
No kernel may reach another device: no remote copies, remote signals or barrier semaphores. Data moves between devices by JAX's collectives and lax.ppermute only.
A program may use at most 64 MiB of HBM per device.

```python
import jax
import jax.numpy as jnp
from jax import lax

LEAF = 256
RANK = 64
LEAVES_DEV = 4
NEAR = 2
FAR = 2
FAR_TOP = 4
MATVECS = 3
BRANCH_LEAVES = 16
NBRANCH = 8
NNODE = 32
NLEAF = 128
N_SUB = 4


def draw_start_vec(key, part):
    rows = jnp.arange(NLEAF, dtype=jnp.float32) / float(NLEAF)
    amplitude = (1.0 + 0.75 * rows)[:, None]
    values = jnp.clip(jax.random.normal(key, (NLEAF, LEAF), jnp.float32), -6.0, 6.0)
    return values * amplitude


def place_ends(array, stream_key, smallest, largest):
    longest = array.shape.index(max(array.shape))
    spots = []
    for shift in (0, 1):
        where = [jax.random.randint(jax.random.fold_in(stream_key, axis), (), 0, length) for axis, length in enumerate(array.shape)]
        where[longest] = (where[longest] + shift) % array.shape[longest]
        spots.append(tuple(where))
    return array.at[spots[0]].set(smallest).at[spots[1]].set(largest)


def level_of(stream_key, shape, shards, least, high):
    level = 1.0
    for dim, blocks in shards:
        heights = jax.random.uniform(jax.random.fold_in(jax.random.fold_in(stream_key, 6), dim), (blocks,), jnp.float32, least / len(shards), high / len(shards))
        level = level * jnp.repeat(jnp.exp(heights), shape[dim] // blocks).reshape((-1,) + (1,) * (len(shape) - 1 - dim))
    return level


def normal_values(own_key, extent, scale, bound, pieces=(), kind=jnp.bfloat16):
    result = scale * jax.random.normal(own_key, extent, jnp.float32)
    if pieces:
        result = result * level_of(own_key, extent, pieces, -0.22, 0.18)
    return jnp.clip(result, -bound, bound).astype(kind)


def setup_inputs(seed: int = 0) -> dict:
    streams_of = jax.random.split(jax.random.key(seed), 11)
    start_vec = draw_start_vec(jax.random.fold_in(streams_of[10], 71), 0)
    near_blocks = normal_values(streams_of[1], (NLEAF, NEAR, LEAF, LEAF), (NEAR * LEAF) ** -0.5, 0.25, ((0, 32),))
    near_ids = place_ends(jax.random.randint(streams_of[2], (NLEAF, NEAR - 1), 0, 3 * BRANCH_LEAVES), jax.random.fold_in(streams_of[2], 1), 0, (3 * BRANCH_LEAVES) - 1).astype(jnp.int32)
    far_ids = place_ends(jax.random.randint(streams_of[3], (NLEAF, FAR), 0, BRANCH_LEAVES), jax.random.fold_in(streams_of[3], 1), 0, BRANCH_LEAVES - 1).astype(jnp.int32)
    leaf_basis = normal_values(streams_of[4], (NLEAF, RANK, LEAF), LEAF ** -0.5, 0.375, ((0, 32),))
    leaf_coupling = normal_values(streams_of[5], (NLEAF, RANK, FAR * RANK), (FAR * RANK) ** -0.5, 0.5, ((0, 32),))
    node_transfer = normal_values(streams_of[6], (NNODE, RANK, LEAVES_DEV * RANK), (LEAVES_DEV * RANK) ** -0.5, 0.375, ((0, 32),))
    branch_transfer = normal_values(streams_of[7], (NNODE, RANK, RANK), RANK ** -0.5, 0.75, ((0, 32),))
    top_ids = place_ends(jax.random.randint(streams_of[8], (NBRANCH, FAR_TOP), 0, NBRANCH), jax.random.fold_in(streams_of[8], 1), 0, NBRANCH - 1).astype(jnp.int32)
    top_coupling = normal_values(streams_of[9], (NBRANCH, RANK, FAR_TOP * RANK), (FAR_TOP * RANK) ** -0.5, 0.375, ((0, 8),))
    return dict(start_vec=start_vec, near_blocks=near_blocks, near_ids=near_ids, far_ids=far_ids, leaf_basis=leaf_basis, leaf_coupling=leaf_coupling, node_transfer=node_transfer, branch_transfer=branch_transfer, top_ids=top_ids, top_coupling=top_coupling)


def apply_matrix(vector, near_blocks, near_ids, far_ids, leaf_basis, leaf_coupling, node_transfer, branch_transfer, top_ids, top_coupling):
    highest = lax.Precision.HIGHEST
    vec_bf = vector.astype(jnp.bfloat16)
    basis_f = leaf_basis.astype(jnp.float32)
    coef_bf = jnp.einsum('lrk,lk->lr', basis_f, vec_bf.astype(jnp.float32)).astype(jnp.bfloat16)
    node_in = coef_bf.reshape(NNODE, LEAVES_DEV * RANK).astype(jnp.float32)
    transfer_f = node_transfer.astype(jnp.float32)
    node_coef = jnp.einsum('nrk,nk->nr', transfer_f, node_in)
    upper_f = branch_transfer.astype(jnp.float32)
    node_term = jnp.einsum('nrs,ns->nr', upper_f, node_coef, precision=highest).astype(jnp.bfloat16)
    branch_coef = lax.optimization_barrier(jnp.sum(node_term.astype(jnp.float32).reshape(NBRANCH, N_SUB, RANK), axis=1)).astype(jnp.bfloat16)
    partners = branch_coef[top_ids].reshape(NBRANCH, FAR_TOP * RANK).astype(jnp.float32)
    branch_local = jnp.einsum('brk,bk->br', top_coupling.astype(jnp.float32), partners)
    node_branch = jnp.repeat(branch_local, N_SUB, axis=0)
    node_local = jnp.einsum('nrs,nr->ns', upper_f, node_branch, precision=highest)
    leaf_down = jnp.einsum('nrk,nr->nk', transfer_f, node_local, precision=highest).reshape(NLEAF, RANK)
    branch_start = jnp.arange(NLEAF, dtype=jnp.int32) // BRANCH_LEAVES * BRANCH_LEAVES
    far_index = (branch_start[:, None] + far_ids).astype(jnp.int32)
    far_coef = coef_bf[far_index].reshape(NLEAF, FAR * RANK).astype(jnp.float32)
    leaf_far = jnp.einsum('lrk,lk->lr', leaf_coupling.astype(jnp.float32), far_coef)
    local_coef = (leaf_down + leaf_far).astype(jnp.bfloat16)
    far_out = jnp.einsum('lrk,lr->lk', basis_f, local_coef.astype(jnp.float32))
    padded = jnp.pad(vec_bf, ((BRANCH_LEAVES, BRANCH_LEAVES), (0, 0)))
    near_index = (branch_start[:, None] + near_ids).astype(jnp.int32)
    picked = padded[near_index]
    near_input = jnp.concatenate([vec_bf[:, None, :], picked], axis=1)
    blocks_grouped = near_blocks.reshape(NBRANCH, BRANCH_LEAVES, NEAR, LEAF, LEAF)
    input_grouped = near_input.reshape(NBRANCH, BRANCH_LEAVES, NEAR, LEAF)

    def branch_near(pair):
        blocks, inputs = pair
        return jnp.einsum('lsij,lsj->li', blocks.astype(jnp.float32), inputs.astype(jnp.float32))
    near_out = lax.map(branch_near, (blocks_grouped, input_grouped)).reshape(NLEAF, LEAF)
    return 0.5 * vector + near_out + far_out

def reference(start_vec, near_blocks, near_ids, far_ids, leaf_basis, leaf_coupling, node_transfer, branch_transfer, top_ids, top_coupling):
    total = float(NLEAF * LEAF)
    first = start_vec * lax.rsqrt(jnp.sum(start_vec * start_vec) / total + 1e-06)
    vectors = [first]
    hessen = jnp.zeros((MATVECS + 1, MATVECS), jnp.float32)
    for column in range(MATVECS):
        image = apply_matrix(vectors[column], near_blocks, near_ids, far_ids, leaf_basis, leaf_coupling, node_transfer, branch_transfer, top_ids, top_coupling)
        dots = jnp.stack([jnp.sum(earlier * image) for earlier in vectors]) / total
        square = jnp.sum(image * image) / total
        remain = square - jnp.sum(dots * dots)
        scale = jnp.sqrt(jnp.maximum(remain, 0.01 * square))
        update = image
        for index_i in range(column + 1):
            update = update - dots[index_i] * vectors[index_i]
        vectors.append(update / scale)
        hessen = hessen.at[:column + 1, column].set(dots)
        hessen = hessen.at[column + 1, column].set(scale)
    return (jnp.stack(vectors), hessen)
```

```python
import jax
import jax.numpy as jnp
from jax import lax
from jax.experimental import pallas as pl
from jax.experimental.pallas import tpu as pltpu
from jax.sharding import PartitionSpec as P

F32 = jnp.float32
BF16 = jnp.bfloat16
ROWS = 8
VMEM = pl.BlockSpec(memory_space=pltpu.VMEM)
SMEM = pl.BlockSpec(memory_space=pltpu.SMEM)


def dot_nt(a, b):
    return lax.dot_general(a, b, (((1,), (1,)), ((), ())), preferred_element_type=F32)


def dot_nn(a, b):
    return lax.dot_general(a, b, (((1,), (0,)), ((), ())), preferred_element_type=F32)


def dot_tn(a, b):
    return lax.dot_general(a, b, (((0,), (0,)), ((), ())), preferred_element_type=F32)


def iota(shape, dim):
    return lax.broadcasted_iota(jnp.int32, shape, dim)


def twice(rows):
    return jnp.concatenate([rows, rows], axis=0)


def by_leaf(parts):
    row = iota(parts[0].shape, 0) % len(parts)
    total = parts[-1]
    for leaf in range(len(parts) - 1):
        total = jnp.where(row == leaf, parts[leaf], total)
    return total


def in_lanes(values):
    group = iota((ROWS, 128), 1) // 32
    out = jnp.zeros((ROWS, 128), F32)
    for index, value in enumerate(values):
        out = jnp.where(group == index, value, out)
    return out


def inner(a, b):
    prod = a * b
    prod = prod[:, :128] + prod[:, 128:]
    return 0.5 * jnp.sum(jnp.sum(prod, axis=0, keepdims=True), axis=1, keepdims=True)


def write_block(vec, dots, basis2_ref, down_ref, out_ref):
    leaves = basis2_ref.shape[0]
    vec_bf = vec.astype(BF16)
    coef = by_leaf([dot_nt(vec_bf, basis2_ref[l]) for l in range(leaves)])
    term = jnp.zeros((ROWS, 128), F32)
    for l in range(leaves):
        one = jnp.broadcast_to(vec[l : l + 1, :], vec.shape).astype(BF16)
        term = term + dot_nt(one, down_ref[l])
    val = in_lanes(dots)
    rest = val - val.astype(BF16).astype(F32)
    last = rest - rest.astype(BF16).astype(F32)
    row = iota((ROWS, 128), 0)
    left = jnp.where(row < 4, vec[:, :128], coef)
    right = jnp.where(row == 4, term, jnp.where(row == 5, val, jnp.where(row == 6, rest, last)))
    right = jnp.where(row < 4, vec[:, 128:], right)
    block = twice(jnp.concatenate([left, right], axis=1)).astype(BF16)
    pairs = out_ref.shape[0] // 16
    if pairs <= 32:
        for p in range(pairs):
            out_ref[16 * p : 16 * p + 16, :] = block
    else:

        def store(p, carry):
            out_ref[pl.ds(pl.multiple_of(16 * p, 16), 16), :] = block
            return carry

        lax.fori_loop(0, pairs, store, 0)


def first_kernel(
    subs,
    near_ids,
    far_ids,
    top_ids,
    place,
    start_ref,
    basis_ref,
    node_ref,
    upper_ref,
    top_ref,
    block_ref,
    pick_ref,
    down_ref,
    top_down_ref,
    basis2_ref,
):
    leaves, rank, _ = basis_ref.shape
    node = node_ref[0]
    reach = dot_nn(upper_ref[0], node).astype(BF16)
    top_down_ref[...] = dot_tn(reach, top_ref[0]).astype(BF16)
    for l in range(leaves):
        own = basis_ref[l]
        basis2_ref[l] = twice(own)
        part = dot_nn(reach[:, l * rank : (l + 1) * rank], own).astype(BF16)
        down_ref[l] = twice(part)
    branch = place[0]
    width = pick_ref.shape[1]
    col = iota((ROWS, width), 1)
    row4 = iota((ROWS, width), 0) % leaves

    def leaf_column(leaf_index, offset):
        return (leaf_index // leaves) * ROWS + leaf_index % leaves + offset

    def pick(columns):
        want = columns[leaves - 1]
        for l in range(leaves - 1):
            want = jnp.where(row4 == l, columns[l], want)
        return (col == want).astype(F32)

    branch_leaves = subs * leaves
    count = (width // ROWS) * leaves
    near = []
    for l in range(leaves):
        index = (branch - 1) * branch_leaves + near_ids[l, 0]
        inside = (index >= 0) & (index < count)
        near.append(jnp.where(inside, leaf_column(jnp.maximum(index, 0), 0), -1))
    groups = [pick(near)]
    for s in range(2):
        groups.append(
            pick([leaf_column(branch * branch_leaves + far_ids[l, s], leaves) for l in range(leaves)])
        )
    for s in range(4):
        groups.append(((col % ROWS == 4) & (col // (ROWS * subs) == top_ids[0, s])).astype(F32))
    groups.append((col % ROWS >= 5).astype(F32))
    pick_ref[...] = jnp.concatenate(groups, axis=0).astype(BF16)
    start = twice(start_ref[...])
    write_block(start, [inner(start, start)], basis2_ref, down_ref, block_ref)


def multiply(own, got_ref, pick_ref, near_ref, top_down_ref, coupling_ref, basis_ref):
    leaves, rank, size = basis_ref.shape
    got = dot_nn(pick_ref[...], got_ref[...])
    group = [got[ROWS * g : ROWS * g + ROWS, :] for g in range(8)]
    low = iota((ROWS, 128), 1) < rank
    far_in = jnp.where(low, group[1][:, :128], group[2][:, :128]).astype(BF16)
    top_a = jnp.where(low, group[3][:, 128:], group[4][:, 128:]).astype(BF16)
    top_b = jnp.where(low, group[5][:, 128:], group[6][:, 128:]).astype(BF16)
    top_in = jnp.concatenate([top_a, top_b], axis=1)
    local = dot_nt(far_in, coupling_ref[...].reshape(leaves * rank, -1))
    local = local + dot_nt(top_in, top_down_ref[...])
    mine = iota((ROWS, leaves * rank), 1) // rank == iota((ROWS, leaves * rank), 0) % leaves
    local = jnp.where(mine, local, 0.0).astype(BF16)
    far_out = dot_nn(local, basis_ref[...].reshape(leaves * rank, size))
    own_bf = own.astype(BF16)
    other = group[0].astype(BF16)
    near_out = by_leaf(
        [dot_nt(own_bf, near_ref[l, 0]) + dot_nt(other, near_ref[l, 1]) for l in range(leaves)]
    )
    dots = [group[7][:, 128 + 32 * i : 129 + 32 * i] for i in range(4)]
    return near_out + far_out, dots


def entry(table, i, j, value):
    row, lane = iota(table.shape, 0), iota(table.shape, 1)
    return jnp.where((row == i) & (lane == j), value, table)


def norm_of(square, heads):
    remain = square
    for head in heads:
        remain = remain - head * head
    return jnp.sqrt(jnp.maximum(remain, 0.01 * square))


def second_kernel(
    total,
    start_ref,
    got_ref,
    pick_ref,
    near_ref,
    top_down_ref,
    coupling_ref,
    basis_ref,
    basis2_ref,
    down_ref,
    block_ref,
    b0_ref,
    k1_ref,
):
    start = twice(start_ref[...])
    image, dots = multiply(
        start, got_ref, pick_ref, near_ref, top_down_ref, coupling_ref, basis_ref
    )
    scale = lax.rsqrt(dots[0] / total + 1e-06)
    b0 = scale * start
    k1 = scale * image
    w0 = 0.5 * b0 + k1
    b0_ref[...] = b0
    k1_ref[...] = k1
    write_block(k1, [inner(b0, w0), inner(w0, w0)], basis2_ref, down_ref, block_ref)


def third_kernel(
    total,
    b0_ref,
    k1_ref,
    got_ref,
    pick_ref,
    near_ref,
    top_down_ref,
    coupling_ref,
    basis_ref,
    basis2_ref,
    down_ref,
    block_ref,
    b1_ref,
    k2_ref,
    table_ref,
):
    k1 = k1_ref[...]
    image, dots = multiply(k1, got_ref, pick_ref, near_ref, top_down_ref, coupling_ref, basis_ref)
    b0 = b0_ref[...]
    h00 = dots[0] / total
    h10 = norm_of(dots[1] / total, [h00])
    inv = 1.0 / h10
    shift = 0.5 - h00
    b1 = (shift * b0 + k1) * inv
    k2 = (shift * k1 + image) * inv
    w1 = 0.5 * b1 + k2
    b1_ref[...] = b1
    k2_ref[...] = k2
    table = jnp.zeros((ROWS, 128), F32)
    table = entry(table, 0, 0, h00)
    table_ref[...] = entry(table, 1, 0, h10)
    write_block(
        k2, [inner(b0, w1), inner(b1, w1), inner(w1, w1)], basis2_ref, down_ref, block_ref
    )


def fourth_kernel(
    total,
    b0_ref,
    k1_ref,
    b1_ref,
    k2_ref,
    table_in_ref,
    got_ref,
    pick_ref,
    near_ref,
    top_down_ref,
    coupling_ref,
    basis_ref,
    dots_ref,
    b2_ref,
    w2_ref,
    table_ref,
):
    k2 = k2_ref[...]
    image, dots = multiply(k2, got_ref, pick_ref, near_ref, top_down_ref, coupling_ref, basis_ref)
    b0, k1, b1 = b0_ref[...], k1_ref[...], b1_ref[...]
    h01 = dots[0] / total
    h11 = dots[1] / total
    h21 = norm_of(dots[2] / total, [h01, h11])
    inv = 1.0 / h21
    shift = 0.5 - h11
    b2 = (shift * b1 + k2 - h01 * b0) * inv
    k3 = (shift * k2 + image - h01 * k1) * inv
    w2 = 0.5 * b2 + k3
    b2_ref[...] = b2
    w2_ref[...] = w2
    table = entry(table_in_ref[...], 0, 1, h01)
    table = entry(table, 1, 1, h11)
    table_ref[...] = entry(table, 2, 1, h21)
    val = in_lanes([inner(b0, w2), inner(b1, w2), inner(b2, w2), inner(w2, w2)])
    dots_ref[...] = jnp.broadcast_to(val[:1, :].reshape(1, 1, 128), dots_ref.shape)


def last_kernel(
    total, b0_ref, b1_ref, b2_ref, w2_ref, table_ref, dots_ref, out_ref, hessen_ref
):
    leaves = out_ref.shape[1]
    sums = jnp.sum(dots_ref[...], axis=0)
    dots = [sums[:, 32 * i : 32 * i + 1] / total for i in range(4)]
    b0, b1, b2 = b0_ref[:leaves, :], b1_ref[:leaves, :], b2_ref[:leaves, :]
    scale = norm_of(dots[3], dots[:3])
    update = w2_ref[:leaves, :] - dots[0] * b0 - dots[1] * b1 - dots[2] * b2
    out_ref[0] = b0
    out_ref[1] = b1
    out_ref[2] = b2
    out_ref[3] = update * (1.0 / scale)
    table = table_ref[...]
    for i in range(3):
        table = entry(table, i, 2, dots[i])
    table = entry(table, 3, 2, scale)
    hessen_ref[...] = table[:4, :3]


def shaped(shape, dtype=F32):
    return jax.ShapeDtypeStruct(shape, dtype)


def call(kernel, ins, outs):
    return pl.pallas_call(
        kernel,
        in_specs=ins,
        out_specs=[VMEM] * len(outs),
        out_shape=outs,
        compiler_params=pltpu.CompilerParams(vmem_limit_bytes=16 * 1024 * 1024),
    )


def per_device(
    start_vec,
    near_blocks,
    near_ids,
    far_ids,
    leaf_basis,
    leaf_coupling,
    node_transfer,
    branch_transfer,
    top_ids,
    top_coupling,
):
    axes = ("leaf", "sub")
    subs = lax.axis_size("sub")
    devices = lax.axis_size("leaf") * subs
    leaves, size = start_vec.shape
    rank = leaf_basis.shape[1]
    total = float(leaves * size * devices)
    block = shaped((devices * ROWS, size), BF16)
    vec = shaped((ROWS, size))
    table = shaped((ROWS, 128))

    def exchange(blocks):
        return lax.all_to_all(blocks, axes, 0, 0, tiled=True)

    place = lax.axis_index("leaf").astype(jnp.int32).reshape(1)
    out, pick, down, top_down, basis2 = call(
        lambda *refs: first_kernel(subs, *refs),
        [SMEM] * 4 + [VMEM] * 5,
        [
            block,
            shaped((8 * ROWS, devices * ROWS), BF16),
            shaped((leaves, 2 * rank, size), BF16),
            shaped((leaves * rank, top_coupling.shape[2]), BF16),
            shaped((leaves, 2 * rank, size), BF16),
        ],
    )(
        near_ids,
        far_ids,
        top_ids,
        place,
        start_vec,
        leaf_basis,
        node_transfer,
        branch_transfer,
        top_coupling,
    )
    fixed = (pick, near_blocks, top_down, leaf_coupling, leaf_basis)
    out, b0, k1 = call(
        lambda *refs: second_kernel(total, *refs), [VMEM] * 9, [block, vec, vec]
    )(start_vec, exchange(out), *fixed, basis2, down)
    out, b1, k2, heads = call(
        lambda *refs: third_kernel(total, *refs), [VMEM] * 10, [block, vec, vec, table]
    )(b0, k1, exchange(out), *fixed, basis2, down)
    dots, b2, w2, heads = call(
        lambda *refs: fourth_kernel(total, *refs),
        [VMEM] * 11,
        [shaped((devices, 1, 128)), vec, vec, table],
    )(b0, k1, b1, k2, heads, exchange(out), *fixed)
    basis, hessen = call(
        lambda *refs: last_kernel(total, *refs),
        [VMEM] * 6,
        [shaped((4, leaves, size)), shaped((4, 3))],
    )(b0, b1, b2, w2, heads, exchange(dots))
    return basis, hessen


def solution(mesh):
    placed = (
        P(("leaf", "sub"), None),
        P(("leaf", "sub"), None, None, None),
        P(("leaf", "sub"), None),
        P(("leaf", "sub"), None),
        P(("leaf", "sub"), None, None),
        P(("leaf", "sub"), None, None),
        P(("leaf", "sub"), None, None),
        P(("leaf", "sub"), None, None),
        P("leaf", None),
        P("leaf", None, None),
    )
    return jax.shard_map(
        per_device,
        mesh=mesh,
        in_specs=placed,
        out_specs=(P(None, ("leaf", "sub"), None), P()),
        check_vma=False,
    )
```

```python
import jax
import jax.numpy as jnp
from jax import lax
from jax.experimental import pallas as pl
from jax.experimental.pallas import tpu as pltpu
from jax.sharding import PartitionSpec as P

F32 = jnp.float32
BF16 = jnp.bfloat16
ROWS = 8
VMEM = pl.BlockSpec(memory_space=pltpu.VMEM)
HBM = pl.BlockSpec(memory_space=pltpu.HBM)


def dot_nt(a, b):
    return lax.dot_general(a, b, (((1,), (1,)), ((), ())), preferred_element_type=F32)


def dot_nn(a, b):
    return lax.dot_general(a, b, (((1,), (0,)), ((), ())), preferred_element_type=F32)


def dot_tn(a, b):
    return lax.dot_general(a, b, (((0,), (0,)), ((), ())), preferred_element_type=F32)


def iota(shape, dim):
    return lax.broadcasted_iota(jnp.int32, shape, dim)


def twice(rows):
    return jnp.concatenate([rows, rows], axis=0)


def by_leaf(parts):
    row = iota(parts[0].shape, 0) % len(parts)
    total = parts[-1]
    for leaf in range(len(parts) - 1):
        total = jnp.where(row == leaf, parts[leaf], total)
    return total


def in_lanes(values):
    group = iota((ROWS, 128), 1) // 32
    out = jnp.zeros((ROWS, 128), F32)
    for index, value in enumerate(values):
        out = jnp.where(group == index, value, out)
    return out


def inner(a, b):
    prod = a * b
    prod = prod[:, :128] + prod[:, 128:]
    return 0.5 * jnp.sum(jnp.sum(prod, axis=0, keepdims=True), axis=1, keepdims=True)


def is_mine(shape, rank, leaves):
    return iota(shape, 1) // rank == iota(shape, 0) % leaves


def make_block(vec, dots, basis, reach2):
    leaves, rank, size = basis.shape
    coef = dot_nt(vec.astype(BF16), basis.reshape(leaves * rank, size))
    coef = jnp.where(is_mine(coef.shape, rank, leaves), coef, 0.0)
    term = 0.5 * jnp.sum(dot_nt(coef.astype(BF16), reach2), axis=0, keepdims=True)
    coef = coef[:, :128] + coef[:, 128:]
    coef = coef + pltpu.roll(coef, rank, 1)
    val = in_lanes(dots)
    rest = val - val.astype(BF16).astype(F32)
    last = rest - rest.astype(BF16).astype(F32)
    row = iota((ROWS, 128), 0)
    left = jnp.where(row < 4, vec[:, :128], coef)
    right = jnp.where(row == 4, term, jnp.where(row == 5, val, jnp.where(row == 6, rest, last)))
    right = jnp.where(row < 4, vec[:, 128:], right)
    return twice(jnp.concatenate([left, right], axis=1)).astype(BF16)


def store_all(block, out_ref):
    pairs = out_ref.shape[0] // 16
    if pairs <= 32:
        for p in range(pairs):
            out_ref[16 * p : 16 * p + 16, :] = block
    else:

        def store(p, carry):
            out_ref[pl.ds(pl.multiple_of(16 * p, 16), 16), :] = block
            return carry

        lax.fori_loop(0, pairs, store, 0)


def first_kernel(
    start_hbm,
    basis_hbm,
    node_hbm,
    upper_hbm,
    block_ref,
    reach2_ref,
    start_ref,
    basis_ref,
    node_ref,
    upper_ref,
    sems,
):
    sources = (basis_hbm, node_hbm, upper_hbm, start_hbm)
    targets = (basis_ref, node_ref, upper_ref, start_ref)
    copies = [
        pltpu.make_async_copy(source, target, sems.at[i])
        for i, (source, target) in enumerate(zip(sources, targets))
    ]
    for copy in copies:
        copy.start()
    for copy in copies:
        copy.wait()
    reach2 = twice(dot_nn(upper_ref[0], node_ref[0])).astype(BF16)
    reach2_ref[...] = reach2
    start = twice(start_ref[...])
    store_all(make_block(start, [inner(start, start)], basis_ref[...], reach2), block_ref)


def own_part(vec, near_ref):
    vec_bf = vec.astype(BF16)
    return by_leaf([dot_nt(vec_bf, near_ref[l, 0]) for l in range(near_ref.shape[0])])


def setup_kernel(
    subs,
    near_ids_ref,
    far_ids_ref,
    top_ids_ref,
    branch_ref,
    reach2_ref,
    top_ref,
    start_ref,
    near_ref,
    pick_ref,
    top_down_ref,
    own_ref,
):
    own_ref[...] = own_part(twice(start_ref[...]), near_ref)
    near_ids, far_ids, top_ids = near_ids_ref[...], far_ids_ref[...], top_ids_ref[...]
    branch = branch_ref[...]
    leaves = near_ids.shape[1]
    rank = top_ref.shape[1]
    top_down_ref[...] = dot_tn(reach2_ref[:rank, :], top_ref[0]).astype(BF16)
    width = pick_ref.shape[1]
    col = iota((ROWS, width), 1)
    lane4, row4 = iota((ROWS, leaves), 1), iota((ROWS, leaves), 0) % leaves

    def by_row(ids):
        kept = jnp.where(lane4 == row4, ids, 0).astype(F32)
        return jnp.sum(kept, axis=1, keepdims=True).astype(jnp.int32)

    def leaf_column(index):
        return 2 * index - index % leaves

    branch_leaves = subs * leaves
    count = (width // ROWS) * leaves
    index = (branch - 1) * branch_leaves + by_row(near_ids)
    inside = (index >= 0) & (index < count)
    groups = [col == jnp.where(inside, leaf_column(jnp.maximum(index, 0)), -1)]
    for s in range(2):
        index = branch * branch_leaves + by_row(far_ids[s : s + 1, :])
        groups.append(col == leaf_column(index) + leaves)
    for s in range(4):
        groups.append((col % ROWS == 4) & (col // (ROWS * subs) == top_ids[0:1, s : s + 1]))
    groups.append(col % ROWS >= 5)
    pick_ref[...] = jnp.concatenate([g.astype(F32) for g in groups], axis=0).astype(BF16)


def multiply(own_out, got_ref, pick_ref, near_ref, top_down_ref, coupling_ref, basis_ref):
    leaves, rank, size = basis_ref.shape
    got = dot_nn(pick_ref[...], got_ref[...])
    group = [got[ROWS * g : ROWS * g + ROWS, :] for g in range(8)]
    low = iota((ROWS, 128), 1) < rank
    far_in = jnp.where(low, group[1][:, :128], group[2][:, :128]).astype(BF16)
    top_a = jnp.where(low, group[3][:, 128:], group[4][:, 128:]).astype(BF16)
    top_b = jnp.where(low, group[5][:, 128:], group[6][:, 128:]).astype(BF16)
    top_in = jnp.concatenate([top_a, top_b], axis=1)
    local = dot_nt(far_in, coupling_ref[...].reshape(leaves * rank, -1))
    local = local + dot_nt(top_in, top_down_ref[...])
    local = jnp.where(is_mine(local.shape, rank, leaves), local, 0.0).astype(BF16)
    far_out = dot_nn(local, basis_ref[...].reshape(leaves * rank, size))
    other = group[0].astype(BF16)
    near_out = own_out + by_leaf([dot_nt(other, near_ref[l, 1]) for l in range(leaves)])
    dots = [group[7][:, 128 + 32 * i : 129 + 32 * i] for i in range(4)]
    return near_out + far_out, dots


def entry(table, i, j, value):
    row, lane = iota(table.shape, 0), iota(table.shape, 1)
    return jnp.where((row == i) & (lane == j), value, table)


def norm_of(square, heads):
    remain = square
    for head in heads:
        remain = remain - head * head
    return jnp.sqrt(jnp.maximum(remain, 0.01 * square))


def second_kernel(
    total,
    start_ref,
    own_ref,
    got_ref,
    pick_ref,
    near_ref,
    top_down_ref,
    coupling_ref,
    basis_ref,
    reach2_ref,
    block_ref,
    b0_ref,
    k1_ref,
):
    start = twice(start_ref[...])
    image, dots = multiply(
        own_ref[...], got_ref, pick_ref, near_ref, top_down_ref, coupling_ref, basis_ref
    )
    scale = lax.rsqrt(dots[0] / total + 1e-06)
    b0 = scale * start
    k1 = scale * image
    w0 = 0.5 * b0 + k1
    b0_ref[...] = b0
    k1_ref[...] = k1
    dots = [inner(b0, w0), inner(w0, w0)]
    store_all(make_block(k1, dots, basis_ref[...], reach2_ref[...]), block_ref)


def third_kernel(
    total,
    b0_ref,
    k1_ref,
    got_ref,
    pick_ref,
    near_ref,
    top_down_ref,
    coupling_ref,
    basis_ref,
    reach2_ref,
    block_ref,
    b1_ref,
    k2_ref,
    table_ref,
):
    k1 = k1_ref[...]
    image, dots = multiply(
        own_part(k1, near_ref),
        got_ref,
        pick_ref,
        near_ref,
        top_down_ref,
        coupling_ref,
        basis_ref,
    )
    b0 = b0_ref[...]
    h00 = dots[0] / total
    h10 = norm_of(dots[1] / total, [h00])
    inv = 1.0 / h10
    shift = 0.5 - h00
    b1 = (shift * b0 + k1) * inv
    k2 = (shift * k1 + image) * inv
    w1 = 0.5 * b1 + k2
    b1_ref[...] = b1
    k2_ref[...] = k2
    table = jnp.zeros((ROWS, 128), F32)
    table = entry(table, 0, 0, h00)
    table_ref[...] = entry(table, 1, 0, h10)
    dots = [inner(b0, w1), inner(b1, w1), inner(w1, w1)]
    store_all(make_block(k2, dots, basis_ref[...], reach2_ref[...]), block_ref)


def fourth_kernel(
    total,
    b0_ref,
    k1_ref,
    b1_ref,
    k2_ref,
    table_in_ref,
    got_ref,
    pick_ref,
    near_ref,
    top_down_ref,
    coupling_ref,
    basis_ref,
    dots_ref,
    b2_ref,
    w2_ref,
    table_ref,
):
    k2 = k2_ref[...]
    image, dots = multiply(
        own_part(k2, near_ref),
        got_ref,
        pick_ref,
        near_ref,
        top_down_ref,
        coupling_ref,
        basis_ref,
    )
    b0, k1, b1 = b0_ref[...], k1_ref[...], b1_ref[...]
    h01 = dots[0] / total
    h11 = dots[1] / total
    h21 = norm_of(dots[2] / total, [h01, h11])
    inv = 1.0 / h21
    shift = 0.5 - h11
    b2 = (shift * b1 + k2 - h01 * b0) * inv
    k3 = (shift * k2 + image - h01 * k1) * inv
    w2 = 0.5 * b2 + k3
    b2_ref[...] = b2
    w2_ref[...] = w2
    table = entry(table_in_ref[...], 0, 1, h01)
    table = entry(table, 1, 1, h11)
    table_ref[...] = entry(table, 2, 1, h21)
    val = in_lanes([inner(b0, w2), inner(b1, w2), inner(b2, w2), inner(w2, w2)])
    dots_ref[...] = jnp.broadcast_to(val[:1, :].reshape(1, 1, 128), dots_ref.shape)


def last_kernel(
    total, b0_ref, b1_ref, b2_ref, w2_ref, table_ref, dots_ref, out_ref, hessen_ref
):
    leaves = out_ref.shape[1]
    sums = jnp.sum(dots_ref[...], axis=0)
    dots = [sums[:, 32 * i : 32 * i + 1] / total for i in range(4)]
    b0, b1, b2 = b0_ref[:leaves, :], b1_ref[:leaves, :], b2_ref[:leaves, :]
    scale = norm_of(dots[3], dots[:3])
    update = w2_ref[:leaves, :] - dots[0] * b0 - dots[1] * b1 - dots[2] * b2
    out_ref[0] = b0
    out_ref[1] = b1
    out_ref[2] = b2
    out_ref[3] = update * (1.0 / scale)
    table = table_ref[...]
    for i in range(3):
        table = entry(table, i, 2, dots[i])
    table = entry(table, 3, 2, scale)
    hessen_ref[...] = table[:4, :3]


def shaped(shape, dtype=F32):
    return jax.ShapeDtypeStruct(shape, dtype)


def call(kernel, ins, outs, scratch=()):
    return pl.pallas_call(
        kernel,
        in_specs=ins,
        out_specs=[VMEM] * len(outs),
        out_shape=outs,
        scratch_shapes=scratch,
        compiler_params=pltpu.CompilerParams(vmem_limit_bytes=16 * 1024 * 1024),
    )


def per_device(
    start_vec,
    near_blocks,
    near_ids,
    far_ids,
    leaf_basis,
    leaf_coupling,
    node_transfer,
    branch_transfer,
    top_ids,
    top_coupling,
):
    axes = ("leaf", "sub")
    subs = lax.axis_size("sub")
    devices = lax.axis_size("leaf") * subs
    leaves, size = start_vec.shape
    rank = leaf_basis.shape[1]
    total = float(leaves * size * devices)
    blocks = shaped((devices * ROWS, size), BF16)
    vec = shaped((ROWS, size))
    table = shaped((ROWS, 128))

    def exchange(out):
        return lax.all_to_all(out, axes, 0, 0, tiled=True)

    sources = (start_vec, leaf_basis, node_transfer, branch_transfer)
    out, reach2 = call(
        first_kernel,
        [HBM] * 4,
        [blocks, shaped((2 * rank, leaves * rank), BF16)],
        [pltpu.VMEM(a.shape, a.dtype) for a in sources] + [pltpu.SemaphoreType.DMA((4,))],
    )(*[pltpu.with_memory_space_constraint(a, pltpu.HBM) for a in sources])
    got = exchange(out)
    branch = lax.axis_index("leaf").astype(jnp.int32).reshape(1, 1)
    pick, top_down, own = call(
        lambda *refs: setup_kernel(subs, *refs),
        [VMEM] * 8,
        [
            shaped((8 * ROWS, devices * ROWS), BF16),
            shaped((leaves * rank, top_coupling.shape[2]), BF16),
            vec,
        ],
    )(near_ids.T, far_ids.T, top_ids, branch, reach2, top_coupling, start_vec, near_blocks)
    fixed = (pick, near_blocks, top_down, leaf_coupling, leaf_basis)
    out, b0, k1 = call(
        lambda *refs: second_kernel(total, *refs), [VMEM] * 9, [blocks, vec, vec]
    )(start_vec, own, got, *fixed, reach2)
    out, b1, k2, heads = call(
        lambda *refs: third_kernel(total, *refs), [VMEM] * 9, [blocks, vec, vec, table]
    )(b0, k1, exchange(out), *fixed, reach2)
    dots, b2, w2, heads = call(
        lambda *refs: fourth_kernel(total, *refs),
        [VMEM] * 11,
        [shaped((devices, 1, 128)), vec, vec, table],
    )(b0, k1, b1, k2, heads, exchange(out), *fixed)
    basis, hessen = call(
        lambda *refs: last_kernel(total, *refs),
        [VMEM] * 6,
        [shaped((4, leaves, size)), shaped((4, 3))],
    )(b0, b1, b2, w2, heads, exchange(dots))
    return basis, hessen


def solution(mesh):
    placed = (
        P(("leaf", "sub"), None),
        P(("leaf", "sub"), None, None, None),
        P(("leaf", "sub"), None),
        P(("leaf", "sub"), None),
        P(("leaf", "sub"), None, None),
        P(("leaf", "sub"), None, None),
        P(("leaf", "sub"), None, None),
        P(("leaf", "sub"), None, None),
        P("leaf", None),
        P("leaf", None, None),
    )
    return jax.shard_map(
        per_device,
        mesh=mesh,
        in_specs=placed,
        out_specs=(P(None, ("leaf", "sub"), None), P()),
        check_vma=False,
    )
```

```python
import jax
import jax.numpy as jnp
from jax import lax
from jax.experimental import pallas as pl
from jax.experimental.pallas import tpu as pltpu
from jax.sharding import PartitionSpec as P

F32 = jnp.float32
BF16 = jnp.bfloat16
ROWS = 8
VMEM = pl.BlockSpec(memory_space=pltpu.VMEM)
HBM = pl.BlockSpec(memory_space=pltpu.HBM)


def dot_nt(a, b):
    return lax.dot_general(a, b, (((1,), (1,)), ((), ())), preferred_element_type=F32)


def dot_nn(a, b):
    return lax.dot_general(a, b, (((1,), (0,)), ((), ())), preferred_element_type=F32)


def dot_tn(a, b):
    return lax.dot_general(a, b, (((0,), (0,)), ((), ())), preferred_element_type=F32)


def iota(shape, dim):
    return lax.broadcasted_iota(jnp.int32, shape, dim)


def twice(rows):
    return jnp.concatenate([rows, rows], axis=0)


def by_leaf(parts):
    row = iota(parts[0].shape, 0) % len(parts)
    total = parts[-1]
    for leaf in range(len(parts) - 1):
        total = jnp.where(row == leaf, parts[leaf], total)
    return total


def in_lanes(values, first, width):
    group = iota((ROWS, 128), 1) // width - first // width
    out = jnp.zeros((ROWS, 128), F32)
    for index, value in enumerate(values):
        out = jnp.where(group == index, value, out)
    return out


def inner(a, b):
    prod = a * b
    prod = prod[:, :128] + prod[:, 128:]
    return 0.5 * jnp.sum(jnp.sum(prod, axis=0, keepdims=True), axis=1, keepdims=True)


def is_mine(shape, rank, leaves):
    return iota(shape, 1) // rank == iota(shape, 0) % leaves


def make_block(vec, dots, basis, reach2):
    leaves, rank, size = basis.shape
    coef = dot_nt(vec.astype(BF16), basis.reshape(leaves * rank, size))
    coef = jnp.where(is_mine(coef.shape, rank, leaves), coef, 0.0)
    term = 0.5 * jnp.sum(dot_nt(coef.astype(BF16), reach2), axis=0, keepdims=True)
    coef = coef[:, :128] + coef[:, 128:]
    coef = coef + pltpu.roll(coef, rank, 1)
    val = in_lanes(dots, rank, 16)
    rest = val - val.astype(BF16).astype(F32)
    last = rest - rest.astype(BF16).astype(F32)
    row, low = iota((ROWS, 128), 0), iota((ROWS, 128), 1) < rank
    third = jnp.where(row == 0, term, jnp.where(row == 1, val, jnp.where(row == 2, rest, last)))
    third = jnp.where(low, coef, third)
    return [part[:leaves, :].astype(BF16) for part in (vec[:, :128], vec[:, 128:], third)]


def store_all(block, out_ref):
    devices = out_ref.shape[0]

    def store(device):
        for part in range(3):
            out_ref[device, part] = block[part]

    if devices <= 32:
        for device in range(devices):
            store(device)
    else:
        pl.loop(0, devices)(store)


def first_kernel(
    start_hbm,
    basis_hbm,
    node_hbm,
    upper_hbm,
    block_ref,
    reach2_ref,
    start_ref,
    basis_ref,
    node_ref,
    upper_ref,
    sems,
):
    sources = (basis_hbm, node_hbm, upper_hbm, start_hbm)
    targets = (basis_ref, node_ref, upper_ref, start_ref)
    copies = [
        pltpu.make_async_copy(source, target, sems.at[i])
        for i, (source, target) in enumerate(zip(sources, targets))
    ]
    for copy in copies:
        copy.start()
    for copy in copies:
        copy.wait()
    reach2 = twice(dot_nn(upper_ref[0], node_ref[0])).astype(BF16)
    reach2_ref[...] = reach2
    start = twice(start_ref[...])
    store_all(make_block(start, [inner(start, start)], basis_ref[...], reach2), block_ref)


def own_part(vec, near_ref):
    vec_bf = vec.astype(BF16)
    return by_leaf([dot_nt(vec_bf, near_ref[l, 0]) for l in range(near_ref.shape[0])])


def setup_kernel(
    subs,
    near_ids_ref,
    far_ids_ref,
    top_ids_ref,
    branch_ref,
    reach2_ref,
    top_ref,
    start_ref,
    near_ref,
    pick_ref,
    top_down_ref,
    own_ref,
):
    own_ref[...] = own_part(twice(start_ref[...]), near_ref)
    near_ids, far_ids, top_ids = near_ids_ref[...], far_ids_ref[...], top_ids_ref[...]
    branch = branch_ref[...]
    leaves = near_ids.shape[1]
    rank = top_ref.shape[1]
    top_down_ref[...] = dot_tn(reach2_ref[:rank, :], top_ref[0]).astype(BF16)
    width = pick_ref.shape[1]
    col = iota((ROWS, width), 1)
    lane4, row4 = iota((ROWS, leaves), 1), iota((ROWS, leaves), 0) % leaves

    def by_row(ids):
        kept = jnp.where(lane4 == row4, ids, 0).astype(F32)
        return jnp.sum(kept, axis=1, keepdims=True).astype(jnp.int32)

    branch_leaves = subs * leaves
    index = (branch - 1) * branch_leaves + by_row(near_ids)
    groups = [col == index]
    for s in range(2):
        groups.append(col == branch * branch_leaves + by_row(far_ids[s : s + 1, :]))
    for s in range(4):
        groups.append((col % leaves == 0) & (col // branch_leaves == top_ids[0:1, s : s + 1]))
    groups.append(col % leaves > 0)
    pick_ref[...] = jnp.concatenate([g.astype(F32) for g in groups], axis=0).astype(BF16)


def multiply(own_out, got_ref, pick_ref, near_ref, top_down_ref, coupling_ref, basis_ref):
    leaves, rank, size = basis_ref.shape
    got = [got_ref[:, part].reshape(-1, 128) for part in range(3)]
    pick = pick_ref[...]
    other = jnp.concatenate([dot_nn(pick[:ROWS], got[0]), dot_nn(pick[:ROWS], got[1])], axis=1)
    rest = dot_nn(pick[ROWS:], got[2])
    group = [rest[ROWS * g : ROWS * g + ROWS, :] for g in range(7)]
    low = iota((ROWS, 128), 1) < rank
    far_in = jnp.where(low, group[0], pltpu.roll(group[1], rank, 1)).astype(BF16)
    top_a = jnp.where(low, pltpu.roll(group[2], rank, 1), group[3]).astype(BF16)
    top_b = jnp.where(low, pltpu.roll(group[4], rank, 1), group[5]).astype(BF16)
    top_in = jnp.concatenate([top_a, top_b], axis=1)
    local = dot_nt(far_in, coupling_ref[...].reshape(leaves * rank, -1))
    local = local + dot_nt(top_in, top_down_ref[...])
    local = jnp.where(is_mine(local.shape, rank, leaves), local, 0.0).astype(BF16)
    far_out = dot_nn(local, basis_ref[...].reshape(leaves * rank, size))
    other = other.astype(BF16)
    near_out = own_out + by_leaf([dot_nt(other, near_ref[l, 1]) for l in range(leaves)])
    dots = [group[6][:, rank + 16 * i : rank + 16 * i + 1] for i in range(4)]
    return near_out + far_out, dots


def entry(table, i, j, value):
    row, lane = iota(table.shape, 0), iota(table.shape, 1)
    return jnp.where((row == i) & (lane == j), value, table)


def norm_of(square, heads):
    remain = square
    for head in heads:
        remain = remain - head * head
    return jnp.sqrt(jnp.maximum(remain, 0.01 * square))


def second_kernel(
    total,
    start_ref,
    own_ref,
    got_ref,
    pick_ref,
    near_ref,
    top_down_ref,
    coupling_ref,
    basis_ref,
    reach2_ref,
    block_ref,
    b0_ref,
    k1_ref,
):
    start = twice(start_ref[...])
    image, dots = multiply(
        own_ref[...], got_ref, pick_ref, near_ref, top_down_ref, coupling_ref, basis_ref
    )
    scale = lax.rsqrt(dots[0] / total + 1e-06)
    b0 = scale * start
    k1 = scale * image
    w0 = 0.5 * b0 + k1
    b0_ref[...] = b0
    k1_ref[...] = k1
    dots = [inner(b0, w0), inner(w0, w0)]
    store_all(make_block(k1, dots, basis_ref[...], reach2_ref[...]), block_ref)


def third_kernel(
    total,
    b0_ref,
    k1_ref,
    got_ref,
    pick_ref,
    near_ref,
    top_down_ref,
    coupling_ref,
    basis_ref,
    reach2_ref,
    block_ref,
    b1_ref,
    k2_ref,
    table_ref,
):
    k1 = k1_ref[...]
    image, dots = multiply(
        own_part(k1, near_ref),
        got_ref,
        pick_ref,
        near_ref,
        top_down_ref,
        coupling_ref,
        basis_ref,
    )
    b0 = b0_ref[...]
    h00 = dots[0] / total
    h10 = norm_of(dots[1] / total, [h00])
    inv = 1.0 / h10
    shift = 0.5 - h00
    b1 = (shift * b0 + k1) * inv
    k2 = (shift * k1 + image) * inv
    w1 = 0.5 * b1 + k2
    b1_ref[...] = b1
    k2_ref[...] = k2
    table = jnp.zeros((ROWS, 128), F32)
    table = entry(table, 0, 0, h00)
    table_ref[...] = entry(table, 1, 0, h10)
    dots = [inner(b0, w1), inner(b1, w1), inner(w1, w1)]
    store_all(make_block(k2, dots, basis_ref[...], reach2_ref[...]), block_ref)


def fourth_kernel(
    total,
    b0_ref,
    k1_ref,
    b1_ref,
    k2_ref,
    table_in_ref,
    got_ref,
    pick_ref,
    near_ref,
    top_down_ref,
    coupling_ref,
    basis_ref,
    dots_ref,
    b2_ref,
    w2_ref,
    table_ref,
):
    k2 = k2_ref[...]
    image, dots = multiply(
        own_part(k2, near_ref),
        got_ref,
        pick_ref,
        near_ref,
        top_down_ref,
        coupling_ref,
        basis_ref,
    )
    b0, k1, b1 = b0_ref[...], k1_ref[...], b1_ref[...]
    h01 = dots[0] / total
    h11 = dots[1] / total
    h21 = norm_of(dots[2] / total, [h01, h11])
    inv = 1.0 / h21
    shift = 0.5 - h11
    b2 = (shift * b1 + k2 - h01 * b0) * inv
    k3 = (shift * k2 + image - h01 * k1) * inv
    w2 = 0.5 * b2 + k3
    b2_ref[...] = b2
    w2_ref[...] = w2
    table = entry(table_in_ref[...], 0, 1, h01)
    table = entry(table, 1, 1, h11)
    table_ref[...] = entry(table, 2, 1, h21)
    val = in_lanes([inner(b0, w2), inner(b1, w2), inner(b2, w2), inner(w2, w2)], 0, 32)
    dots_ref[...] = jnp.broadcast_to(val[:1, :].reshape(1, 1, 128), dots_ref.shape)


def last_kernel(
    total, b0_ref, b1_ref, b2_ref, w2_ref, table_ref, dots_ref, out_ref, hessen_ref
):
    leaves = out_ref.shape[1]
    sums = jnp.sum(dots_ref[...], axis=0)
    dots = [sums[:, 32 * i : 32 * i + 1] / total for i in range(4)]
    b0, b1, b2 = b0_ref[:leaves, :], b1_ref[:leaves, :], b2_ref[:leaves, :]
    scale = norm_of(dots[3], dots[:3])
    update = w2_ref[:leaves, :] - dots[0] * b0 - dots[1] * b1 - dots[2] * b2
    out_ref[0] = b0
    out_ref[1] = b1
    out_ref[2] = b2
    out_ref[3] = update * (1.0 / scale)
    table = table_ref[...]
    for i in range(3):
        table = entry(table, i, 2, dots[i])
    table = entry(table, 3, 2, scale)
    hessen_ref[...] = table[:4, :3]


def shaped(shape, dtype=F32):
    return jax.ShapeDtypeStruct(shape, dtype)


def call(kernel, ins, outs, scratch=()):
    return pl.pallas_call(
        kernel,
        in_specs=ins,
        out_specs=[VMEM] * len(outs),
        out_shape=outs,
        scratch_shapes=scratch,
        compiler_params=pltpu.CompilerParams(vmem_limit_bytes=16 * 1024 * 1024),
    )


def per_device(
    start_vec,
    near_blocks,
    near_ids,
    far_ids,
    leaf_basis,
    leaf_coupling,
    node_transfer,
    branch_transfer,
    top_ids,
    top_coupling,
):
    axes = ("leaf", "sub")
    subs = lax.axis_size("sub")
    devices = lax.axis_size("leaf") * subs
    leaves, size = start_vec.shape
    rank = leaf_basis.shape[1]
    total = float(leaves * size * devices)
    blocks = shaped((devices, 3, leaves, size // 2), BF16)
    vec = shaped((ROWS, size))
    table = shaped((ROWS, 128))

    def exchange(out):
        return lax.all_to_all(out, axes, 0, 0, tiled=True)

    sources = (start_vec, leaf_basis, node_transfer, branch_transfer)
    out, reach2 = call(
        first_kernel,
        [HBM] * 4,
        [blocks, shaped((2 * rank, leaves * rank), BF16)],
        [pltpu.VMEM(a.shape, a.dtype) for a in sources] + [pltpu.SemaphoreType.DMA((4,))],
    )(*[pltpu.with_memory_space_constraint(a, pltpu.HBM) for a in sources])
    got = exchange(out)
    branch = lax.axis_index("leaf").astype(jnp.int32).reshape(1, 1)
    pick, top_down, own = call(
        lambda *refs: setup_kernel(subs, *refs),
        [VMEM] * 8,
        [
            shaped((8 * ROWS, devices * leaves), BF16),
            shaped((leaves * rank, top_coupling.shape[2]), BF16),
            vec,
        ],
    )(near_ids.T, far_ids.T, top_ids, branch, reach2, top_coupling, start_vec, near_blocks)
    fixed = (pick, near_blocks, top_down, leaf_coupling, leaf_basis)
    out, b0, k1 = call(
        lambda *refs: second_kernel(total, *refs), [VMEM] * 9, [blocks, vec, vec]
    )(start_vec, own, got, *fixed, reach2)
    out, b1, k2, heads = call(
        lambda *refs: third_kernel(total, *refs), [VMEM] * 9, [blocks, vec, vec, table]
    )(b0, k1, exchange(out), *fixed, reach2)
    dots, b2, w2, heads = call(
        lambda *refs: fourth_kernel(total, *refs),
        [VMEM] * 11,
        [shaped((devices, 1, 128)), vec, vec, table],
    )(b0, k1, b1, k2, heads, exchange(out), *fixed)
    basis, hessen = call(
        lambda *refs: last_kernel(total, *refs),
        [VMEM] * 6,
        [shaped((4, leaves, size)), shaped((4, 3))],
    )(b0, b1, b2, w2, heads, exchange(dots))
    return basis, hessen


def solution(mesh):
    placed = (
        P(("leaf", "sub"), None),
        P(("leaf", "sub"), None, None, None),
        P(("leaf", "sub"), None),
        P(("leaf", "sub"), None),
        P(("leaf", "sub"), None, None),
        P(("leaf", "sub"), None, None),
        P(("leaf", "sub"), None, None),
        P(("leaf", "sub"), None, None),
        P("leaf", None),
        P("leaf", None, None),
    )
    return jax.shard_map(
        per_device,
        mesh=mesh,
        in_specs=placed,
        out_specs=(P(None, ("leaf", "sub"), None), P()),
        check_vma=False,
    )
```

```python
import jax
import jax.numpy as jnp
from jax import lax
from jax.experimental import pallas as pl
from jax.experimental.pallas import tpu as pltpu
from jax.sharding import PartitionSpec as P

F32 = jnp.float32
BF16 = jnp.bfloat16
ROWS = 8
VMEM = pl.BlockSpec(memory_space=pltpu.VMEM)
HBM = pl.BlockSpec(memory_space=pltpu.HBM)


def dot_nt(a, b):
    return lax.dot_general(a, b, (((1,), (1,)), ((), ())), preferred_element_type=F32)


def dot_nn(a, b):
    return lax.dot_general(a, b, (((1,), (0,)), ((), ())), preferred_element_type=F32)


def dot_tn(a, b):
    return lax.dot_general(a, b, (((0,), (0,)), ((), ())), preferred_element_type=F32)


def iota(shape, dim):
    return lax.broadcasted_iota(jnp.int32, shape, dim)


def twice(rows):
    return jnp.concatenate([rows, rows], axis=0)


def by_leaf(parts):
    row = iota(parts[0].shape, 0) % len(parts)
    total = parts[-1]
    for leaf in range(len(parts) - 1):
        total = jnp.where(row == leaf, parts[leaf], total)
    return total


def in_lanes(values, first, width):
    group = iota((ROWS, 128), 1) // width - first // width
    out = jnp.zeros((ROWS, 128), F32)
    for index, value in enumerate(values):
        out = jnp.where(group == index, value, out)
    return out


def inner(a, b):
    prod = a * b
    prod = prod[:, :128] + prod[:, 128:]
    return 0.5 * jnp.sum(jnp.sum(prod, axis=0, keepdims=True), axis=1, keepdims=True)


def is_mine(shape, rank, leaves):
    return iota(shape, 1) // rank == iota(shape, 0) % leaves


def make_block(vec, dots, basis, reach2):
    leaves, rank, size = basis.shape
    coef = dot_nt(vec.astype(BF16), basis.reshape(leaves * rank, size))
    coef = jnp.where(is_mine(coef.shape, rank, leaves), coef, 0.0)
    term = 0.5 * jnp.sum(dot_nt(coef.astype(BF16), reach2), axis=0, keepdims=True)
    coef = coef[:, :128] + coef[:, 128:]
    coef = coef + pltpu.roll(coef, rank, 1)
    val = in_lanes(dots, rank, 16)
    rest = val - val.astype(BF16).astype(F32)
    last = rest - rest.astype(BF16).astype(F32)
    row, low = iota((ROWS, 128), 0), iota((ROWS, 128), 1) < rank
    third = jnp.where(row == 0, term, jnp.where(row == 1, val, jnp.where(row == 2, rest, last)))
    third = jnp.where(low, coef, third)
    return [part[:leaves, :].astype(BF16) for part in (vec[:, :128], vec[:, 128:], third)]


def store_all(block, out_ref):
    devices = out_ref.shape[0]

    def store(device):
        for part in range(3):
            out_ref[device, part] = block[part]

    if devices <= 32:
        for device in range(devices):
            store(device)
    else:
        pl.loop(0, devices)(store)


def first_kernel(
    start_hbm,
    basis_hbm,
    node_hbm,
    upper_hbm,
    block_ref,
    reach2_ref,
    start_ref,
    basis_ref,
    node_ref,
    upper_ref,
    sems,
):
    sources = (basis_hbm, node_hbm, upper_hbm, start_hbm)
    targets = (basis_ref, node_ref, upper_ref, start_ref)
    copies = [
        pltpu.make_async_copy(source, target, sems.at[i])
        for i, (source, target) in enumerate(zip(sources, targets))
    ]
    for copy in copies:
        copy.start()
    for copy in copies:
        copy.wait()
    reach2 = twice(dot_nn(upper_ref[0], node_ref[0])).astype(BF16)
    reach2_ref[...] = reach2
    start = twice(start_ref[...])
    store_all(make_block(start, [inner(start, start)], basis_ref[...], reach2), block_ref)


def own_part(vec, near_ref):
    vec_bf = vec.astype(BF16)
    return by_leaf([dot_nt(vec_bf, near_ref[l, 0]) for l in range(near_ref.shape[0])])


def setup_kernel(
    subs,
    near_ids_ref,
    far_ids_ref,
    top_ids_ref,
    branch_ref,
    reach2_ref,
    top_ref,
    start_ref,
    near_ref,
    pick_ref,
    top_down_ref,
    own_ref,
):
    own_ref[...] = own_part(twice(start_ref[...]), near_ref)
    near_ids, far_ids, top_ids = near_ids_ref[...], far_ids_ref[...], top_ids_ref[...]
    branch = branch_ref[...]
    leaves = near_ids.shape[1]
    rank = top_ref.shape[1]
    top_down_ref[...] = dot_tn(reach2_ref[:rank, :], top_ref[0]).astype(BF16)
    width = pick_ref.shape[1]
    col = iota((ROWS, width), 1)
    lane4, row4 = iota((ROWS, leaves), 1), iota((ROWS, leaves), 0) % leaves

    def by_row(ids):
        kept = jnp.where(lane4 == row4, ids, 0).astype(F32)
        return jnp.sum(kept, axis=1, keepdims=True).astype(jnp.int32)

    branch_leaves = subs * leaves
    index = (branch - 1) * branch_leaves + by_row(near_ids)
    groups = [col == index]
    for s in range(2):
        groups.append(col == branch * branch_leaves + by_row(far_ids[s : s + 1, :]))
    for s in range(4):
        groups.append((col % leaves == 0) & (col // branch_leaves == top_ids[0:1, s : s + 1]))
    groups.append(col % leaves > 0)
    pick_ref[...] = jnp.concatenate([g.astype(F32) for g in groups], axis=0).astype(BF16)


def multiply(own, got_ref, pick_ref, near_ref, top_down_ref, coupling_ref, basis_ref):
    leaves, rank, size = basis_ref.shape
    got = [got_ref[:, part].reshape(-1, 128) for part in range(3)]
    pick = pick_ref[...]
    rest = dot_nn(pick[ROWS:], got[2])
    other = jnp.concatenate([dot_nn(pick[:ROWS], got[0]), dot_nn(pick[:ROWS], got[1])], axis=1)
    near_out = own()
    group = [rest[ROWS * g : ROWS * g + ROWS, :] for g in range(7)]
    low = iota((ROWS, 128), 1) < rank
    far_in = jnp.where(low, group[0], pltpu.roll(group[1], rank, 1)).astype(BF16)
    top_a = jnp.where(low, pltpu.roll(group[2], rank, 1), group[3]).astype(BF16)
    top_b = jnp.where(low, pltpu.roll(group[4], rank, 1), group[5]).astype(BF16)
    top_in = jnp.concatenate([top_a, top_b], axis=1)
    local = dot_nt(far_in, coupling_ref[...].reshape(leaves * rank, -1))
    local = local + dot_nt(top_in, top_down_ref[...])
    other = other.astype(BF16)
    near_out = near_out + by_leaf([dot_nt(other, near_ref[l, 1]) for l in range(leaves)])
    local = jnp.where(is_mine(local.shape, rank, leaves), local, 0.0).astype(BF16)
    far_out = dot_nn(local, basis_ref[...].reshape(leaves * rank, size))
    dots = [group[6][:, rank + 16 * i : rank + 16 * i + 1] for i in range(4)]
    return near_out + far_out, dots


def entry(table, i, j, value):
    row, lane = iota(table.shape, 0), iota(table.shape, 1)
    return jnp.where((row == i) & (lane == j), value, table)


def norm_of(square, heads):
    remain = square
    for head in heads:
        remain = remain - head * head
    remain = jnp.maximum(remain, 0.01 * square)
    return jnp.sqrt(remain), lax.rsqrt(remain)


def second_kernel(
    total,
    start_ref,
    own_ref,
    got_ref,
    pick_ref,
    near_ref,
    top_down_ref,
    coupling_ref,
    basis_ref,
    reach2_ref,
    block_ref,
    b0_ref,
    k1_ref,
):
    start = twice(start_ref[...])
    image, dots = multiply(
        lambda: own_ref[...], got_ref, pick_ref, near_ref, top_down_ref, coupling_ref, basis_ref
    )
    scale = lax.rsqrt(dots[0] * (1.0 / total) + 1e-06)
    b0 = scale * start
    k1 = scale * image
    w0 = 0.5 * b0 + k1
    b0_ref[...] = b0
    k1_ref[...] = k1
    dots = [inner(b0, w0), inner(w0, w0)]
    store_all(make_block(k1, dots, basis_ref[...], reach2_ref[...]), block_ref)


def third_kernel(
    total,
    b0_ref,
    k1_ref,
    got_ref,
    pick_ref,
    near_ref,
    top_down_ref,
    coupling_ref,
    basis_ref,
    reach2_ref,
    block_ref,
    b1_ref,
    k2_ref,
    table_ref,
):
    k1 = k1_ref[...]
    image, dots = multiply(
        lambda: own_part(k1, near_ref),
        got_ref,
        pick_ref,
        near_ref,
        top_down_ref,
        coupling_ref,
        basis_ref,
    )
    b0 = b0_ref[...]
    h00 = dots[0] * (1.0 / total)
    h10, inv = norm_of(dots[1] * (1.0 / total), [h00])
    shift = 0.5 - h00
    b1 = (shift * b0 + k1) * inv
    k2 = (shift * k1 + image) * inv
    w1 = 0.5 * b1 + k2
    b1_ref[...] = b1
    k2_ref[...] = k2
    table = jnp.zeros((ROWS, 128), F32)
    table = entry(table, 0, 0, h00)
    table_ref[...] = entry(table, 1, 0, h10)
    dots = [inner(b0, w1), inner(b1, w1), inner(w1, w1)]
    store_all(make_block(k2, dots, basis_ref[...], reach2_ref[...]), block_ref)


def fourth_kernel(
    total,
    b0_ref,
    k1_ref,
    b1_ref,
    k2_ref,
    table_in_ref,
    got_ref,
    pick_ref,
    near_ref,
    top_down_ref,
    coupling_ref,
    basis_ref,
    dots_ref,
    b2_ref,
    w2_ref,
    table_ref,
):
    k2 = k2_ref[...]
    image, dots = multiply(
        lambda: own_part(k2, near_ref),
        got_ref,
        pick_ref,
        near_ref,
        top_down_ref,
        coupling_ref,
        basis_ref,
    )
    b0, k1, b1 = b0_ref[...], k1_ref[...], b1_ref[...]
    h01 = dots[0] * (1.0 / total)
    h11 = dots[1] * (1.0 / total)
    h21, inv = norm_of(dots[2] * (1.0 / total), [h01, h11])
    shift = 0.5 - h11
    b2 = (shift * b1 + k2 - h01 * b0) * inv
    k3 = (shift * k2 + image - h01 * k1) * inv
    w2 = 0.5 * b2 + k3
    b2_ref[...] = b2
    w2_ref[...] = w2
    table = entry(table_in_ref[...], 0, 1, h01)
    table = entry(table, 1, 1, h11)
    table_ref[...] = entry(table, 2, 1, h21)
    val = in_lanes([inner(b0, w2), inner(b1, w2), inner(b2, w2), inner(w2, w2)], 0, 32)
    dots_ref[...] = jnp.broadcast_to(val[:1, :].reshape(1, 1, 128), dots_ref.shape)


def last_kernel(
    total, b0_ref, b1_ref, b2_ref, w2_ref, table_ref, dots_ref, out_ref, hessen_ref
):
    leaves = out_ref.shape[1]
    sums = jnp.sum(dots_ref[...], axis=0) * (1.0 / total)
    dots = [sums[:, 32 * i : 32 * i + 1] for i in range(4)]
    b0, b1, b2 = b0_ref[:leaves, :], b1_ref[:leaves, :], b2_ref[:leaves, :]
    scale, inv = norm_of(dots[3], dots[:3])
    update = w2_ref[:leaves, :] - dots[0] * b0 - dots[1] * b1 - dots[2] * b2
    out_ref[0] = b0
    out_ref[1] = b1
    out_ref[2] = b2
    out_ref[3] = update * inv
    table = table_ref[...]
    for i in range(3):
        table = entry(table, i, 2, dots[i])
    table = entry(table, 3, 2, scale)
    hessen_ref[...] = table[:4, :3]


def shaped(shape, dtype=F32):
    return jax.ShapeDtypeStruct(shape, dtype)


def call(kernel, ins, outs, scratch=()):
    return pl.pallas_call(
        kernel,
        in_specs=ins,
        out_specs=[VMEM] * len(outs),
        out_shape=outs,
        scratch_shapes=scratch,
        compiler_params=pltpu.CompilerParams(vmem_limit_bytes=16 * 1024 * 1024),
    )


def per_device(
    start_vec,
    near_blocks,
    near_ids,
    far_ids,
    leaf_basis,
    leaf_coupling,
    node_transfer,
    branch_transfer,
    top_ids,
    top_coupling,
):
    axes = ("leaf", "sub")
    subs = lax.axis_size("sub")
    devices = lax.axis_size("leaf") * subs
    leaves, size = start_vec.shape
    rank = leaf_basis.shape[1]
    total = float(leaves * size * devices)
    blocks = shaped((devices, 3, leaves, size // 2), BF16)
    vec = shaped((ROWS, size))
    table = shaped((ROWS, 128))

    def exchange(out):
        return lax.all_to_all(out, axes, 0, 0, tiled=True)

    sources = (start_vec, leaf_basis, node_transfer, branch_transfer)
    out, reach2 = call(
        first_kernel,
        [HBM] * 4,
        [blocks, shaped((2 * rank, leaves * rank), BF16)],
        [pltpu.VMEM(a.shape, a.dtype) for a in sources] + [pltpu.SemaphoreType.DMA((4,))],
    )(*[pltpu.with_memory_space_constraint(a, pltpu.HBM) for a in sources])
    got = exchange(out)
    branch = lax.axis_index("leaf").astype(jnp.int32).reshape(1, 1)
    pick, top_down, own = call(
        lambda *refs: setup_kernel(subs, *refs),
        [VMEM] * 8,
        [
            shaped((8 * ROWS, devices * leaves), BF16),
            shaped((leaves * rank, top_coupling.shape[2]), BF16),
            vec,
        ],
    )(near_ids.T, far_ids.T, top_ids, branch, reach2, top_coupling, start_vec, near_blocks)
    fixed = (pick, near_blocks, top_down, leaf_coupling, leaf_basis)
    out, b0, k1 = call(
        lambda *refs: second_kernel(total, *refs), [VMEM] * 9, [blocks, vec, vec]
    )(start_vec, own, got, *fixed, reach2)
    out, b1, k2, heads = call(
        lambda *refs: third_kernel(total, *refs), [VMEM] * 9, [blocks, vec, vec, table]
    )(b0, k1, exchange(out), *fixed, reach2)
    dots, b2, w2, heads = call(
        lambda *refs: fourth_kernel(total, *refs),
        [VMEM] * 11,
        [shaped((devices, 1, 128)), vec, vec, table],
    )(b0, k1, b1, k2, heads, exchange(out), *fixed)
    basis, hessen = call(
        lambda *refs: last_kernel(total, *refs),
        [VMEM] * 6,
        [shaped((4, leaves, size)), shaped((4, 3))],
    )(b0, b1, b2, w2, heads, exchange(dots))
    return basis, hessen


def solution(mesh):
    placed = (
        P(("leaf", "sub"), None),
        P(("leaf", "sub"), None, None, None),
        P(("leaf", "sub"), None),
        P(("leaf", "sub"), None),
        P(("leaf", "sub"), None, None),
        P(("leaf", "sub"), None, None),
        P(("leaf", "sub"), None, None),
        P(("leaf", "sub"), None, None),
        P("leaf", None),
        P("leaf", None, None),
    )
    return jax.shard_map(
        per_device,
        mesh=mesh,
        in_specs=placed,
        out_specs=(P(None, ("leaf", "sub"), None), P()),
        check_vma=False,
    )
```

```python
import jax
import jax.numpy as jnp
from jax import lax
from jax.experimental import pallas as pl
from jax.experimental.pallas import tpu as pltpu
from jax.sharding import PartitionSpec as P

F32 = jnp.float32
BF16 = jnp.bfloat16
ROWS = 8
VMEM = pl.BlockSpec(memory_space=pltpu.VMEM)
HBM = pl.BlockSpec(memory_space=pltpu.HBM)


def dot_nt(a, b):
    return lax.dot_general(a, b, (((1,), (1,)), ((), ())), preferred_element_type=F32)


def dot_nn(a, b):
    return lax.dot_general(a, b, (((1,), (0,)), ((), ())), preferred_element_type=F32)


def dot_tn(a, b):
    return lax.dot_general(a, b, (((0,), (0,)), ((), ())), preferred_element_type=F32)


def iota(shape, dim):
    return lax.broadcasted_iota(jnp.int32, shape, dim)


def twice(rows):
    return jnp.concatenate([rows, rows], axis=0)


def by_leaf(parts):
    row = iota(parts[0].shape, 0) % len(parts)
    total = parts[-1]
    for leaf in range(len(parts) - 1):
        total = jnp.where(row == leaf, parts[leaf], total)
    return total


def in_lanes(values, first, width):
    group = iota((ROWS, 128), 1) // width - first // width
    out = jnp.zeros((ROWS, 128), F32)
    for index, value in enumerate(values):
        out = jnp.where(group == index, value, out)
    return out


def inner(a, b):
    prod = a * b
    prod = prod[:, :128] + prod[:, 128:]
    return 0.5 * jnp.sum(jnp.sum(prod, axis=0, keepdims=True), axis=1, keepdims=True)


def is_mine(shape, rank, leaves):
    return iota(shape, 1) // rank == iota(shape, 0) % leaves


def make_block(vec, dots, basis, reach2):
    leaves, rank, size = basis.shape
    coef = dot_nt(vec.astype(BF16), basis.reshape(leaves * rank, size))
    coef = jnp.where(is_mine(coef.shape, rank, leaves), coef, 0.0)
    term = 0.5 * jnp.sum(dot_nt(coef.astype(BF16), reach2), axis=0, keepdims=True)
    coef = coef[:, :128] + coef[:, 128:]
    coef = coef + pltpu.roll(coef, rank, 1)
    val = in_lanes(dots, rank, 16)
    rest = val - val.astype(BF16).astype(F32)
    last = rest - rest.astype(BF16).astype(F32)
    row, low = iota((ROWS, 128), 0), iota((ROWS, 128), 1) < rank
    third = jnp.where(row == 0, term, jnp.where(row == 1, val, jnp.where(row == 2, rest, last)))
    third = jnp.where(low, coef, third)
    return [part[:leaves, :].astype(BF16) for part in (vec[:, :128], vec[:, 128:], third)]


def store_all(block, out_ref):
    devices = out_ref.shape[0]

    def store(device):
        for part in range(3):
            out_ref[device, part] = block[part]

    if devices <= 32:
        for device in range(devices):
            store(device)
    else:
        pl.loop(0, devices)(store)


def first_kernel(
    start_hbm,
    basis_hbm,
    node_hbm,
    upper_hbm,
    block_ref,
    reach2_ref,
    start_ref,
    basis_ref,
    node_ref,
    upper_ref,
    sems,
):
    sources = (basis_hbm, node_hbm, upper_hbm, start_hbm)
    targets = (basis_ref, node_ref, upper_ref, start_ref)
    copies = [
        pltpu.make_async_copy(source, target, sems.at[i])
        for i, (source, target) in enumerate(zip(sources, targets))
    ]
    for copy in copies:
        copy.start()
    for copy in copies:
        copy.wait()
    reach2 = twice(dot_nn(upper_ref[0], node_ref[0])).astype(BF16)
    reach2_ref[...] = reach2
    start = twice(start_ref[...])
    store_all(make_block(start, [inner(start, start)], basis_ref[...], reach2), block_ref)


def own_part(vec, near_ref):
    vec_bf = vec.astype(BF16)
    return by_leaf([dot_nt(vec_bf, near_ref[l, 0]) for l in range(near_ref.shape[0])])


def setup_kernel(
    subs,
    near_ids_ref,
    far_ids_ref,
    top_ids_ref,
    branch_ref,
    reach2_ref,
    top_ref,
    start_ref,
    near_ref,
    pick_ref,
    top_down_ref,
    own_ref,
):
    own_ref[...] = own_part(twice(start_ref[...]), near_ref)
    near_ids, far_ids, top_ids = near_ids_ref[...], far_ids_ref[...], top_ids_ref[...]
    branch = branch_ref[...]
    leaves = near_ids.shape[1]
    rank = top_ref.shape[1]
    top_down_ref[...] = dot_tn(reach2_ref[:rank, :], top_ref[0]).astype(BF16)
    width = pick_ref.shape[1]
    col = iota((ROWS, width), 1)
    lane4, row4 = iota((ROWS, leaves), 1), iota((ROWS, leaves), 0) % leaves

    def by_row(ids):
        kept = jnp.where(lane4 == row4, ids, 0).astype(F32)
        return jnp.sum(kept, axis=1, keepdims=True).astype(jnp.int32)

    branches = width // (subs * leaves)

    def column(at, index):
        return ((index // leaves) * branches + at) * leaves + index % leaves

    ids = by_row(near_ids)
    at = branch - 1 + ids // (subs * leaves)
    inside = (at >= 0) & (at < branches)
    groups = [col == jnp.where(inside, column(at, ids % (subs * leaves)), -1)]
    for s in range(2):
        groups.append(col == column(branch, by_row(far_ids[s : s + 1, :])))
    for s in range(4):
        at = (col // leaves) % branches
        groups.append((col % leaves == 0) & (at == top_ids[0:1, s : s + 1]))
    groups.append(col % leaves > 0)
    pick_ref[...] = jnp.concatenate([g.astype(F32) for g in groups], axis=0).astype(BF16)


def multiply(own, got_ref, pick_ref, near_ref, top_down_ref, coupling_ref, basis_ref):
    leaves, rank, size = basis_ref.shape
    got = [got_ref[:, part].reshape(-1, 128) for part in range(3)]
    pick = pick_ref[...]
    rest = dot_nn(pick[ROWS:], got[2])
    other = jnp.concatenate([dot_nn(pick[:ROWS], got[0]), dot_nn(pick[:ROWS], got[1])], axis=1)
    near_out = own()
    group = [rest[ROWS * g : ROWS * g + ROWS, :] for g in range(7)]
    low = iota((ROWS, 128), 1) < rank
    far_in = jnp.where(low, group[0], pltpu.roll(group[1], rank, 1)).astype(BF16)
    top_a = jnp.where(low, pltpu.roll(group[2], rank, 1), group[3]).astype(BF16)
    top_b = jnp.where(low, pltpu.roll(group[4], rank, 1), group[5]).astype(BF16)
    top_in = jnp.concatenate([top_a, top_b], axis=1)
    local = dot_nt(far_in, coupling_ref[...].reshape(leaves * rank, -1))
    local = local + dot_nt(top_in, top_down_ref[...])
    other = other.astype(BF16)
    near_out = near_out + by_leaf([dot_nt(other, near_ref[l, 1]) for l in range(leaves)])
    local = jnp.where(is_mine(local.shape, rank, leaves), local, 0.0).astype(BF16)
    far_out = dot_nn(local, basis_ref[...].reshape(leaves * rank, size))
    dots = [group[6][:, rank + 16 * i : rank + 16 * i + 1] for i in range(4)]
    return near_out + far_out, dots


def entry(table, i, j, value):
    row, lane = iota(table.shape, 0), iota(table.shape, 1)
    return jnp.where((row == i) & (lane == j), value, table)


def norm_of(square, heads):
    remain = square
    for head in heads:
        remain = remain - head * head
    remain = jnp.maximum(remain, 0.01 * square)
    return jnp.sqrt(remain), lax.rsqrt(remain)


def second_kernel(
    total,
    start_ref,
    own_ref,
    got_ref,
    pick_ref,
    near_ref,
    top_down_ref,
    coupling_ref,
    basis_ref,
    reach2_ref,
    block_ref,
    b0_ref,
    k1_ref,
):
    start = twice(start_ref[...])
    image, dots = multiply(
        lambda: own_ref[...], got_ref, pick_ref, near_ref, top_down_ref, coupling_ref, basis_ref
    )
    scale = lax.rsqrt(dots[0] * (1.0 / total) + 1e-06)
    b0 = scale * start
    k1 = scale * image
    w0 = 0.5 * b0 + k1
    b0_ref[...] = b0
    k1_ref[...] = k1
    dots = [inner(b0, w0), inner(w0, w0)]
    store_all(make_block(k1, dots, basis_ref[...], reach2_ref[...]), block_ref)


def third_kernel(
    total,
    b0_ref,
    k1_ref,
    got_ref,
    pick_ref,
    near_ref,
    top_down_ref,
    coupling_ref,
    basis_ref,
    reach2_ref,
    block_ref,
    b1_ref,
    k2_ref,
    table_ref,
):
    k1 = k1_ref[...]
    image, dots = multiply(
        lambda: own_part(k1, near_ref),
        got_ref,
        pick_ref,
        near_ref,
        top_down_ref,
        coupling_ref,
        basis_ref,
    )
    b0 = b0_ref[...]
    h00 = dots[0] * (1.0 / total)
    h10, inv = norm_of(dots[1] * (1.0 / total), [h00])
    shift = 0.5 - h00
    b1 = (shift * b0 + k1) * inv
    k2 = (shift * k1 + image) * inv
    w1 = 0.5 * b1 + k2
    b1_ref[...] = b1
    k2_ref[...] = k2
    table = jnp.zeros((ROWS, 128), F32)
    table = entry(table, 0, 0, h00)
    table_ref[...] = entry(table, 1, 0, h10)
    dots = [inner(b0, w1), inner(b1, w1), inner(w1, w1)]
    store_all(make_block(k2, dots, basis_ref[...], reach2_ref[...]), block_ref)


def fourth_kernel(
    total,
    b0_ref,
    k1_ref,
    b1_ref,
    k2_ref,
    table_in_ref,
    got_ref,
    pick_ref,
    near_ref,
    top_down_ref,
    coupling_ref,
    basis_ref,
    dots_ref,
    b2_ref,
    w2_ref,
    table_ref,
):
    k2 = k2_ref[...]
    image, dots = multiply(
        lambda: own_part(k2, near_ref),
        got_ref,
        pick_ref,
        near_ref,
        top_down_ref,
        coupling_ref,
        basis_ref,
    )
    b0, k1, b1 = b0_ref[...], k1_ref[...], b1_ref[...]
    h01 = dots[0] * (1.0 / total)
    h11 = dots[1] * (1.0 / total)
    h21, inv = norm_of(dots[2] * (1.0 / total), [h01, h11])
    shift = 0.5 - h11
    b2 = (shift * b1 + k2 - h01 * b0) * inv
    k3 = (shift * k2 + image - h01 * k1) * inv
    w2 = 0.5 * b2 + k3
    b2_ref[...] = b2
    w2_ref[...] = w2
    table = entry(table_in_ref[...], 0, 1, h01)
    table = entry(table, 1, 1, h11)
    table_ref[...] = entry(table, 2, 1, h21)
    val = in_lanes([inner(b0, w2), inner(b1, w2), inner(b2, w2), inner(w2, w2)], 0, 32)
    dots_ref[...] = jnp.broadcast_to(val[:1, :].reshape(1, 1, 128), dots_ref.shape)


def last_kernel(
    total, b0_ref, b1_ref, b2_ref, w2_ref, table_ref, dots_ref, out_ref, hessen_ref
):
    leaves = out_ref.shape[1]
    sums = jnp.sum(dots_ref[...], axis=0) * (1.0 / total)
    dots = [sums[:, 32 * i : 32 * i + 1] for i in range(4)]
    b0, b1, b2 = b0_ref[:leaves, :], b1_ref[:leaves, :], b2_ref[:leaves, :]
    scale, inv = norm_of(dots[3], dots[:3])
    update = w2_ref[:leaves, :] - dots[0] * b0 - dots[1] * b1 - dots[2] * b2
    out_ref[0] = b0
    out_ref[1] = b1
    out_ref[2] = b2
    out_ref[3] = update * inv
    table = table_ref[...]
    for i in range(3):
        table = entry(table, i, 2, dots[i])
    table = entry(table, 3, 2, scale)
    hessen_ref[...] = table[:4, :3]


def shaped(shape, dtype=F32):
    return jax.ShapeDtypeStruct(shape, dtype)


def call(kernel, ins, outs, scratch=()):
    return pl.pallas_call(
        kernel,
        in_specs=ins,
        out_specs=[VMEM] * len(outs),
        out_shape=outs,
        scratch_shapes=scratch,
        compiler_params=pltpu.CompilerParams(vmem_limit_bytes=16 * 1024 * 1024),
    )


def per_device(
    start_vec,
    near_blocks,
    near_ids,
    far_ids,
    leaf_basis,
    leaf_coupling,
    node_transfer,
    branch_transfer,
    top_ids,
    top_coupling,
):
    subs = lax.axis_size("sub")
    devices = lax.axis_size("leaf") * subs
    leaves, size = start_vec.shape
    rank = leaf_basis.shape[1]
    total = float(leaves * size * devices)
    blocks = shaped((devices, 3, leaves, size // 2), BF16)
    vec = shaped((ROWS, size))
    table = shaped((ROWS, 128))

    def exchange(out):
        return lax.all_to_all(out, ("sub", "leaf"), 0, 0, tiled=True)

    sources = (start_vec, leaf_basis, node_transfer, branch_transfer)
    out, reach2 = call(
        first_kernel,
        [HBM] * 4,
        [blocks, shaped((2 * rank, leaves * rank), BF16)],
        [pltpu.VMEM(a.shape, a.dtype) for a in sources] + [pltpu.SemaphoreType.DMA((4,))],
    )(*[pltpu.with_memory_space_constraint(a, pltpu.HBM) for a in sources])
    got = exchange(out)
    branch = lax.axis_index("leaf").astype(jnp.int32).reshape(1, 1)
    pick, top_down, own = call(
        lambda *refs: setup_kernel(subs, *refs),
        [VMEM] * 8,
        [
            shaped((8 * ROWS, devices * leaves), BF16),
            shaped((leaves * rank, top_coupling.shape[2]), BF16),
            vec,
        ],
    )(near_ids.T, far_ids.T, top_ids, branch, reach2, top_coupling, start_vec, near_blocks)
    fixed = (pick, near_blocks, top_down, leaf_coupling, leaf_basis)
    out, b0, k1 = call(
        lambda *refs: second_kernel(total, *refs), [VMEM] * 9, [blocks, vec, vec]
    )(start_vec, own, got, *fixed, reach2)
    out, b1, k2, heads = call(
        lambda *refs: third_kernel(total, *refs), [VMEM] * 9, [blocks, vec, vec, table]
    )(b0, k1, exchange(out), *fixed, reach2)
    dots, b2, w2, heads = call(
        lambda *refs: fourth_kernel(total, *refs),
        [VMEM] * 11,
        [shaped((devices, 1, 128)), vec, vec, table],
    )(b0, k1, b1, k2, heads, exchange(out), *fixed)
    basis, hessen = call(
        lambda *refs: last_kernel(total, *refs),
        [VMEM] * 6,
        [shaped((4, leaves, size)), shaped((4, 3))],
    )(b0, b1, b2, w2, heads, exchange(dots))
    return basis, hessen


def solution(mesh):
    placed = (
        P(("leaf", "sub"), None),
        P(("leaf", "sub"), None, None, None),
        P(("leaf", "sub"), None),
        P(("leaf", "sub"), None),
        P(("leaf", "sub"), None, None),
        P(("leaf", "sub"), None, None),
        P(("leaf", "sub"), None, None),
        P(("leaf", "sub"), None, None),
        P("leaf", None),
        P("leaf", None, None),
    )
    return jax.shard_map(
        per_device,
        mesh=mesh,
        in_specs=placed,
        out_specs=(P(None, ("leaf", "sub"), None), P()),
        check_vma=False,
    )
```

```python
import jax
import jax.numpy as jnp
from jax import lax
from jax.experimental import pallas as pl
from jax.experimental.pallas import tpu as pltpu
from jax.sharding import PartitionSpec as P

F32 = jnp.float32
BF16 = jnp.bfloat16
ROWS = 8
VMEM = pl.BlockSpec(memory_space=pltpu.VMEM)
HBM = pl.BlockSpec(memory_space=pltpu.HBM)


def dot_nt(a, b):
    return lax.dot_general(a, b, (((1,), (1,)), ((), ())), preferred_element_type=F32)


def dot_nn(a, b):
    return lax.dot_general(a, b, (((1,), (0,)), ((), ())), preferred_element_type=F32)


def dot_tn(a, b):
    return lax.dot_general(a, b, (((0,), (0,)), ((), ())), preferred_element_type=F32)


def iota(shape, dim):
    return lax.broadcasted_iota(jnp.int32, shape, dim)


def twice(rows):
    return jnp.concatenate([rows, rows], axis=0)


def by_leaf(parts):
    row = iota(parts[0].shape, 0) % len(parts)
    total = parts[-1]
    for leaf in range(len(parts) - 1):
        total = jnp.where(row == leaf, parts[leaf], total)
    return total


def in_lanes(values, first, width):
    group = iota((ROWS, 128), 1) // width - first // width
    out = jnp.zeros((ROWS, 128), F32)
    for index, value in enumerate(values):
        out = jnp.where(group == index, value, out)
    return out


def inner(a, b):
    prod = a * b
    prod = prod[:, :128] + prod[:, 128:]
    return 0.5 * jnp.sum(jnp.sum(prod, axis=0, keepdims=True), axis=1, keepdims=True)


def is_mine(shape, rank, leaves):
    return iota(shape, 1) // rank == iota(shape, 0) % leaves


def make_block(vec, dots, basis, reach2):
    leaves, rank, size = basis.shape
    coef = dot_nt(vec.astype(BF16), basis.reshape(leaves * rank, size))
    coef = jnp.where(is_mine(coef.shape, rank, leaves), coef, 0.0)
    term = 0.5 * jnp.sum(dot_nt(coef.astype(BF16), reach2), axis=0, keepdims=True)
    coef = coef[:, :128] + coef[:, 128:]
    coef = coef + pltpu.roll(coef, rank, 1)
    val = in_lanes(dots, rank, 16)
    rest = val - val.astype(BF16).astype(F32)
    last = rest - rest.astype(BF16).astype(F32)
    row, low = iota((ROWS, 128), 0), iota((ROWS, 128), 1) < rank
    third = jnp.where(row == 0, term, jnp.where(row == 1, val, jnp.where(row == 2, rest, last)))
    third = jnp.where(low, coef, third)
    return [part[:leaves, :].astype(BF16) for part in (vec[:, :128], vec[:, 128:], third)]


def store_all(block, out_ref):
    devices = out_ref.shape[0]

    def store(device):
        for part in range(3):
            out_ref[device, part] = block[part]

    if devices <= 32:
        for device in range(devices):
            store(device)
    else:
        pl.loop(0, devices)(store)


def first_kernel(
    subs,
    start_hbm,
    basis_hbm,
    node_hbm,
    upper_hbm,
    top_hbm,
    near_ids_hbm,
    far_ids_hbm,
    top_ids_hbm,
    block_ref,
    reach2_ref,
    start2_ref,
    pick_ref,
    top_down_ref,
    start_ref,
    basis_ref,
    node_ref,
    upper_ref,
    top_ref,
    near_ids_ref,
    far_ids_ref,
    top_ids_ref,
    sems,
):
    pairs = (
        (basis_hbm, basis_ref),
        (near_ids_hbm, near_ids_ref),
        (far_ids_hbm, far_ids_ref),
        (top_ids_hbm, top_ids_ref),
        (node_hbm, node_ref),
        (upper_hbm, upper_ref),
        (top_hbm, top_ref),
        (start_hbm, start_ref),
    )
    copies = [
        pltpu.make_async_copy(source, target, sems.at[i])
        for i, (source, target) in enumerate(pairs)
    ]
    for copy in copies:
        copy.start()
    for copy in copies:
        copy.wait()
    set_picks(subs, near_ids_ref[...], far_ids_ref[...], top_ids_ref[...], pick_ref)
    reach = dot_nn(upper_ref[0], node_ref[0])
    reach2 = twice(reach).astype(BF16)
    reach2_ref[...] = reach2
    start = twice(start_ref[...])
    start2_ref[...] = start
    store_all(make_block(start, [inner(start, start)], basis_ref[...], reach2), block_ref)
    top_down_ref[...] = dot_tn(reach.astype(BF16), top_ref[0]).astype(BF16)


def own_part(vec, near_ref):
    vec_bf = vec.astype(BF16)
    return by_leaf([dot_nt(vec_bf, near_ref[l, 0]) for l in range(near_ref.shape[0])])


def set_picks(subs, near_ids, far_ids, top_ids, pick_ref):
    branch = lax.axis_index("leaf").astype(jnp.int32)
    leaves = near_ids.shape[1]
    width = pick_ref.shape[1]
    col = iota((ROWS, width), 1)
    lane4, row4 = iota((ROWS, leaves), 1), iota((ROWS, leaves), 0) % leaves

    def by_row(ids):
        kept = jnp.where(lane4 == row4, ids, 0).astype(F32)
        return jnp.sum(kept, axis=1, keepdims=True).astype(jnp.int32)

    branches = width // (subs * leaves)

    def column(at, index):
        return ((index // leaves) * branches + at) * leaves + index % leaves

    ids = by_row(near_ids)
    at = branch - 1 + ids // (subs * leaves)
    inside = (at >= 0) & (at < branches)
    groups = [col == jnp.where(inside, column(at, ids % (subs * leaves)), -1)]
    for s in range(2):
        groups.append(col == column(branch, by_row(far_ids[s : s + 1, :])))
    for s in range(4):
        at = (col // leaves) % branches
        groups.append((col % leaves == 0) & (at == top_ids[0:1, s : s + 1]))
    groups.append(col % leaves > 0)
    pick_ref[...] = jnp.concatenate([g.astype(F32) for g in groups], axis=0).astype(BF16)


def multiply(own, got_ref, pick_ref, near_ref, top_down_ref, coupling_ref, basis_ref):
    leaves, rank, size = basis_ref.shape
    got = [got_ref[:, part].reshape(-1, 128) for part in range(3)]
    pick = pick_ref[...]
    rest = dot_nn(pick[ROWS:], got[2])
    other = jnp.concatenate([dot_nn(pick[:ROWS], got[0]), dot_nn(pick[:ROWS], got[1])], axis=1)
    near_out = own()
    group = [rest[ROWS * g : ROWS * g + ROWS, :] for g in range(7)]
    low = iota((ROWS, 128), 1) < rank
    far_in = jnp.where(low, group[0], pltpu.roll(group[1], rank, 1)).astype(BF16)
    top_a = jnp.where(low, pltpu.roll(group[2], rank, 1), group[3]).astype(BF16)
    top_b = jnp.where(low, pltpu.roll(group[4], rank, 1), group[5]).astype(BF16)
    top_in = jnp.concatenate([top_a, top_b], axis=1)
    local = dot_nt(far_in, coupling_ref[...].reshape(leaves * rank, -1))
    local = local + dot_nt(top_in, top_down_ref[...])
    other = other.astype(BF16)
    near_out = near_out + by_leaf([dot_nt(other, near_ref[l, 1]) for l in range(leaves)])
    local = jnp.where(is_mine(local.shape, rank, leaves), local, 0.0).astype(BF16)
    far_out = dot_nn(local, basis_ref[...].reshape(leaves * rank, size))
    dots = [group[6][:, rank + 16 * i : rank + 16 * i + 1] for i in range(4)]
    return near_out + far_out, dots


def entry(table, i, j, value):
    row, lane = iota(table.shape, 0), iota(table.shape, 1)
    return jnp.where((row == i) & (lane == j), value, table)


def norm_of(square, heads):
    remain = square
    for head in heads:
        remain = remain - head * head
    remain = jnp.maximum(remain, 0.01 * square)
    return jnp.sqrt(remain), lax.rsqrt(remain)


def second_kernel(
    total,
    start2_ref,
    got_ref,
    pick_ref,
    near_ref,
    top_down_ref,
    coupling_ref,
    basis_ref,
    reach2_ref,
    block_ref,
    b0_ref,
    k1_ref,
):
    start = start2_ref[...]
    image, dots = multiply(
        lambda: own_part(start, near_ref), got_ref, pick_ref, near_ref, top_down_ref, coupling_ref, basis_ref
    )
    scale = lax.rsqrt(dots[0] * (1.0 / total) + 1e-06)
    b0 = scale * start
    k1 = scale * image
    w0 = 0.5 * b0 + k1
    b0_ref[...] = b0
    k1_ref[...] = k1
    dots = [inner(b0, w0), inner(w0, w0)]
    store_all(make_block(k1, dots, basis_ref[...], reach2_ref[...]), block_ref)


def third_kernel(
    total,
    b0_ref,
    k1_ref,
    got_ref,
    pick_ref,
    near_ref,
    top_down_ref,
    coupling_ref,
    basis_ref,
    reach2_ref,
    block_ref,
    b1_ref,
    k2_ref,
    table_ref,
):
    k1 = k1_ref[...]
    image, dots = multiply(
        lambda: own_part(k1, near_ref),
        got_ref,
        pick_ref,
        near_ref,
        top_down_ref,
        coupling_ref,
        basis_ref,
    )
    b0 = b0_ref[...]
    h00 = dots[0] * (1.0 / total)
    h10, inv = norm_of(dots[1] * (1.0 / total), [h00])
    shift = 0.5 - h00
    b1 = (shift * b0 + k1) * inv
    k2 = (shift * k1 + image) * inv
    w1 = 0.5 * b1 + k2
    b1_ref[...] = b1
    k2_ref[...] = k2
    table = jnp.zeros((ROWS, 128), F32)
    table = entry(table, 0, 0, h00)
    table_ref[...] = entry(table, 1, 0, h10)
    dots = [inner(b0, w1), inner(b1, w1), inner(w1, w1)]
    store_all(make_block(k2, dots, basis_ref[...], reach2_ref[...]), block_ref)


def fourth_kernel(
    total,
    b0_ref,
    k1_ref,
    b1_ref,
    k2_ref,
    table_in_ref,
    got_ref,
    pick_ref,
    near_ref,
    top_down_ref,
    coupling_ref,
    basis_ref,
    dots_ref,
    b2_ref,
    w2_ref,
    table_ref,
):
    k2 = k2_ref[...]
    image, dots = multiply(
        lambda: own_part(k2, near_ref),
        got_ref,
        pick_ref,
        near_ref,
        top_down_ref,
        coupling_ref,
        basis_ref,
    )
    b0, k1, b1 = b0_ref[...], k1_ref[...], b1_ref[...]
    h01 = dots[0] * (1.0 / total)
    h11 = dots[1] * (1.0 / total)
    h21, inv = norm_of(dots[2] * (1.0 / total), [h01, h11])
    shift = 0.5 - h11
    b2 = (shift * b1 + k2 - h01 * b0) * inv
    k3 = (shift * k2 + image - h01 * k1) * inv
    w2 = 0.5 * b2 + k3
    b2_ref[...] = b2
    w2_ref[...] = w2
    table = entry(table_in_ref[...], 0, 1, h01)
    table = entry(table, 1, 1, h11)
    table_ref[...] = entry(table, 2, 1, h21)
    val = in_lanes([inner(b0, w2), inner(b1, w2), inner(b2, w2), inner(w2, w2)], 0, 32)
    dots_ref[...] = jnp.broadcast_to(val[:1, :].reshape(1, 1, 128), dots_ref.shape)


def last_kernel(
    total, b0_ref, b1_ref, b2_ref, w2_ref, table_ref, dots_ref, out_ref, hessen_ref
):
    leaves = out_ref.shape[1]
    sums = jnp.sum(dots_ref[...], axis=0) * (1.0 / total)
    dots = [sums[:, 32 * i : 32 * i + 1] for i in range(4)]
    b0, b1, b2 = b0_ref[:leaves, :], b1_ref[:leaves, :], b2_ref[:leaves, :]
    scale, inv = norm_of(dots[3], dots[:3])
    update = w2_ref[:leaves, :] - dots[0] * b0 - dots[1] * b1 - dots[2] * b2
    out_ref[0] = b0
    out_ref[1] = b1
    out_ref[2] = b2
    out_ref[3] = update * inv
    table = table_ref[...]
    for i in range(3):
        table = entry(table, i, 2, dots[i])
    table = entry(table, 3, 2, scale)
    hessen_ref[...] = table[:4, :3]


def shaped(shape, dtype=F32):
    return jax.ShapeDtypeStruct(shape, dtype)


def call(kernel, ins, outs, scratch=(), cost=None):
    return pl.pallas_call(
        kernel,
        in_specs=ins,
        out_specs=[VMEM] * len(outs),
        out_shape=outs,
        scratch_shapes=scratch,
        cost_estimate=cost,
        compiler_params=pltpu.CompilerParams(vmem_limit_bytes=16 * 1024 * 1024),
    )


def per_device(
    start_vec,
    near_blocks,
    near_ids,
    far_ids,
    leaf_basis,
    leaf_coupling,
    node_transfer,
    branch_transfer,
    top_ids,
    top_coupling,
):
    subs = lax.axis_size("sub")
    devices = lax.axis_size("leaf") * subs
    leaves, size = start_vec.shape
    rank = leaf_basis.shape[1]
    total = float(leaves * size * devices)
    blocks = shaped((devices, 3, leaves, size // 2), BF16)
    vec = shaped((ROWS, size))
    table = shaped((ROWS, 128))

    def exchange(out):
        return lax.all_to_all(out, ("sub", "leaf"), 0, 0, tiled=True)

    sources = (
        start_vec,
        leaf_basis,
        node_transfer,
        branch_transfer,
        top_coupling,
        near_ids.T,
        far_ids.T,
        top_ids,
    )
    out, reach2, start2, pick, top_down = call(
        lambda *refs: first_kernel(subs, *refs),
        [HBM] * len(sources),
        [
            blocks,
            shaped((2 * rank, leaves * rank), BF16),
            vec,
            shaped((8 * ROWS, devices * leaves), BF16),
            shaped((leaves * rank, top_coupling.shape[2]), BF16),
        ],
        [pltpu.VMEM(a.shape, a.dtype) for a in sources]
        + [pltpu.SemaphoreType.DMA((len(sources),))],
        pl.CostEstimate(flops=10000000, bytes_accessed=20000000, transcendentals=0),
    )(*[pltpu.with_memory_space_constraint(a, pltpu.HBM) for a in sources])
    fixed = (pick, near_blocks, top_down, leaf_coupling, leaf_basis)
    out, b0, k1 = call(
        lambda *refs: second_kernel(total, *refs), [VMEM] * 8, [blocks, vec, vec]
    )(start2, exchange(out), *fixed, reach2)
    out, b1, k2, heads = call(
        lambda *refs: third_kernel(total, *refs), [VMEM] * 9, [blocks, vec, vec, table]
    )(b0, k1, exchange(out), *fixed, reach2)
    dots, b2, w2, heads = call(
        lambda *refs: fourth_kernel(total, *refs),
        [VMEM] * 11,
        [shaped((devices, 1, 128)), vec, vec, table],
    )(b0, k1, b1, k2, heads, exchange(out), *fixed)
    basis, hessen = call(
        lambda *refs: last_kernel(total, *refs),
        [VMEM] * 6,
        [shaped((4, leaves, size)), shaped((4, 3))],
    )(b0, b1, b2, w2, heads, exchange(dots))
    return basis, hessen


def solution(mesh):
    placed = (
        P(("leaf", "sub"), None),
        P(("leaf", "sub"), None, None, None),
        P(("leaf", "sub"), None),
        P(("leaf", "sub"), None),
        P(("leaf", "sub"), None, None),
        P(("leaf", "sub"), None, None),
        P(("leaf", "sub"), None, None),
        P(("leaf", "sub"), None, None),
        P("leaf", None),
        P("leaf", None, None),
    )
    return jax.shard_map(
        per_device,
        mesh=mesh,
        in_specs=placed,
        out_specs=(P(None, ("leaf", "sub"), None), P()),
        check_vma=False,
    )
```

```python
import jax
import jax.numpy as jnp
from jax import lax
from jax.experimental import pallas as pl
from jax.experimental.pallas import tpu as pltpu
from jax.sharding import PartitionSpec as P

F32 = jnp.float32
BF16 = jnp.bfloat16
ROWS = 8
VMEM = pl.BlockSpec(memory_space=pltpu.VMEM)
HBM = pl.BlockSpec(memory_space=pltpu.HBM)


def dot_nt(a, b):
    return lax.dot_general(a, b, (((1,), (1,)), ((), ())), preferred_element_type=F32)


def dot_nn(a, b):
    return lax.dot_general(a, b, (((1,), (0,)), ((), ())), preferred_element_type=F32)


def dot_tn(a, b):
    return lax.dot_general(a, b, (((0,), (0,)), ((), ())), preferred_element_type=F32)


def iota(shape, dim):
    return lax.broadcasted_iota(jnp.int32, shape, dim)


def twice(rows):
    return jnp.concatenate([rows, rows], axis=0)


def by_leaf(parts):
    row = iota(parts[0].shape, 0) % len(parts)
    total = parts[-1]
    for leaf in range(len(parts) - 1):
        total = jnp.where(row == leaf, parts[leaf], total)
    return total


def in_lanes(values, first, width):
    group = iota((ROWS, 128), 1) // width - first // width
    out = jnp.zeros((ROWS, 128), F32)
    for index, value in enumerate(values):
        out = jnp.where(group == index, value, out)
    return out


def inner(a, b):
    prod = a * b
    prod = prod[:, :128] + prod[:, 128:]
    return 0.5 * jnp.sum(jnp.sum(prod, axis=0, keepdims=True), axis=1, keepdims=True)


def is_mine(shape, rank, leaves):
    return iota(shape, 1) // rank == iota(shape, 0) % leaves


def make_block(vec, dots, basis, reach2):
    leaves, rank, size = basis.shape
    coef = dot_nt(vec.astype(BF16), basis.reshape(leaves * rank, size))
    coef = jnp.where(is_mine(coef.shape, rank, leaves), coef, 0.0)
    term = 0.5 * jnp.sum(dot_nt(coef.astype(BF16), reach2), axis=0, keepdims=True)
    coef = coef[:, :128] + coef[:, 128:]
    coef = coef + pltpu.roll(coef, rank, 1)
    val = in_lanes(dots, rank, 16)
    rest = val - val.astype(BF16).astype(F32)
    last = rest - rest.astype(BF16).astype(F32)
    row, low = iota((ROWS, 128), 0), iota((ROWS, 128), 1) < rank
    third = jnp.where(row == 0, term, jnp.where(row == 1, val, jnp.where(row == 2, rest, last)))
    third = jnp.where(low, coef, third)
    return [part[:leaves, :].astype(BF16) for part in (vec[:, :128], vec[:, 128:], third)]


def store_all(block, out_ref):
    devices = out_ref.shape[0]

    def store(device):
        for part in range(3):
            out_ref[device, part] = block[part]

    if devices <= 32:
        for device in range(devices):
            store(device)
    else:
        pl.loop(0, devices)(store)


def first_kernel(
    subs,
    start_hbm,
    basis_hbm,
    node_hbm,
    upper_hbm,
    top_hbm,
    near_ids_hbm,
    far_ids_hbm,
    top_ids_hbm,
    block_ref,
    reach2_ref,
    start2_ref,
    pick_ref,
    top_down_ref,
    start_ref,
    basis_ref,
    node_ref,
    upper_ref,
    top_ref,
    near_ids_ref,
    far_ids_ref,
    top_ids_ref,
    sems,
):
    pairs = (
        (basis_hbm, basis_ref),
        (near_ids_hbm, near_ids_ref),
        (far_ids_hbm, far_ids_ref),
        (top_ids_hbm, top_ids_ref),
        (node_hbm, node_ref),
        (upper_hbm, upper_ref),
        (top_hbm, top_ref),
        (start_hbm, start_ref),
    )
    copies = [
        pltpu.make_async_copy(source, target, sems.at[i])
        for i, (source, target) in enumerate(pairs)
    ]
    for copy in copies:
        copy.start()
    for copy in copies:
        copy.wait()
    set_picks(subs, near_ids_ref[...], far_ids_ref[...], top_ids_ref[...], pick_ref)
    reach = dot_nn(upper_ref[0], node_ref[0])
    reach2 = twice(reach).astype(BF16)
    reach2_ref[...] = reach2
    start = twice(start_ref[...])
    start2_ref[...] = start
    store_all(make_block(start, [inner(start, start)], basis_ref[...], reach2), block_ref)
    top_down_ref[...] = dot_tn(reach.astype(BF16), top_ref[0]).astype(BF16)


def own_part(vec, near_ref):
    vec_bf = vec.astype(BF16)
    return by_leaf([dot_nt(vec_bf, near_ref[l, 0]) for l in range(near_ref.shape[0])])


def set_picks(subs, near_ids, far_ids, top_ids, pick_ref):
    branch = lax.axis_index("leaf").astype(jnp.int32)
    leaves = near_ids.shape[1]
    width = pick_ref.shape[1]
    col = iota((ROWS, width), 1)
    lane4, row4 = iota((ROWS, leaves), 1), iota((ROWS, leaves), 0) % leaves

    def by_row(ids):
        kept = jnp.where(lane4 == row4, ids, 0).astype(F32)
        return jnp.sum(kept, axis=1, keepdims=True).astype(jnp.int32)

    branches = width // (subs * leaves)

    def column(at, index):
        return ((index // leaves) * branches + at) * leaves + index % leaves

    ids = by_row(near_ids)
    at = branch - 1 + ids // (subs * leaves)
    inside = (at >= 0) & (at < branches)
    groups = [col == jnp.where(inside, column(at, ids % (subs * leaves)), -1)]
    for s in range(2):
        groups.append(col == column(branch, by_row(far_ids[s : s + 1, :])))
    for s in range(4):
        at = (col // leaves) % branches
        groups.append((col % leaves == 0) & (at == top_ids[0:1, s : s + 1]))
    groups.append(col % leaves > 0)
    pick_ref[...] = jnp.concatenate([g.astype(F32) for g in groups], axis=0).astype(BF16)


def multiply(own, got_ref, pick_ref, near_ref, top_down_ref, coupling_ref, basis_ref):
    leaves, rank, size = basis_ref.shape
    got = [got_ref[:, part].reshape(-1, 128) for part in range(3)]
    pick = pick_ref[...]
    rest = dot_nn(pick[ROWS:], got[2])
    other = jnp.concatenate([dot_nn(pick[:ROWS], got[0]), dot_nn(pick[:ROWS], got[1])], axis=1)
    near_out = own()
    group = [rest[ROWS * g : ROWS * g + ROWS, :] for g in range(7)]
    low = iota((ROWS, 128), 1) < rank
    far_in = jnp.where(low, group[0], pltpu.roll(group[1], rank, 1)).astype(BF16)
    top_a = jnp.where(low, pltpu.roll(group[2], rank, 1), group[3]).astype(BF16)
    top_b = jnp.where(low, pltpu.roll(group[4], rank, 1), group[5]).astype(BF16)
    top_in = jnp.concatenate([top_a, top_b], axis=1)
    local = dot_nt(far_in, coupling_ref[...].reshape(leaves * rank, -1))
    local = local + dot_nt(top_in, top_down_ref[...])
    other = other.astype(BF16)
    near_out = near_out + by_leaf([dot_nt(other, near_ref[l, 1]) for l in range(leaves)])
    local = jnp.where(is_mine(local.shape, rank, leaves), local, 0.0).astype(BF16)
    far_out = dot_nn(local, basis_ref[...].reshape(leaves * rank, size))
    dots = [group[6][:, rank + 16 * i : rank + 16 * i + 1] for i in range(4)]
    return near_out + far_out, dots


def entry(table, i, j, value):
    row, lane = iota(table.shape, 0), iota(table.shape, 1)
    return jnp.where((row == i) & (lane == j), value, table)


def norm_of(square, heads):
    remain = square
    for head in heads:
        remain = remain - head * head
    remain = jnp.maximum(remain, 0.01 * square)
    return jnp.sqrt(remain), lax.rsqrt(remain)


def second_kernel(
    total,
    start2_ref,
    got_ref,
    pick_ref,
    near_ref,
    top_down_ref,
    coupling_ref,
    basis_ref,
    reach2_ref,
    block_ref,
    b0_ref,
    k1_ref,
):
    start = start2_ref[...]
    image, dots = multiply(
        lambda: own_part(start, near_ref), got_ref, pick_ref, near_ref, top_down_ref, coupling_ref, basis_ref
    )
    scale = lax.rsqrt(dots[0] * (1.0 / total) + 1e-06)
    b0 = scale * start
    k1 = scale * image
    w0 = 0.5 * b0 + k1
    b0_ref[...] = b0
    k1_ref[...] = k1
    dots = [inner(b0, w0), inner(w0, w0)]
    store_all(make_block(k1, dots, basis_ref[...], reach2_ref[...]), block_ref)


def third_kernel(
    total,
    b0_ref,
    k1_ref,
    got_ref,
    pick_ref,
    near_ref,
    top_down_ref,
    coupling_ref,
    basis_ref,
    reach2_ref,
    block_ref,
    b1_ref,
    k2_ref,
    table_ref,
):
    k1 = k1_ref[...]
    image, dots = multiply(
        lambda: own_part(k1, near_ref),
        got_ref,
        pick_ref,
        near_ref,
        top_down_ref,
        coupling_ref,
        basis_ref,
    )
    b0 = b0_ref[...]
    h00 = dots[0] * (1.0 / total)
    h10, inv = norm_of(dots[1] * (1.0 / total), [h00])
    shift = 0.5 - h00
    b1 = (shift * b0 + k1) * inv
    k2 = (shift * k1 + image) * inv
    w1 = 0.5 * b1 + k2
    b1_ref[...] = b1
    k2_ref[...] = k2
    table = jnp.zeros((ROWS, 128), F32)
    table = entry(table, 0, 0, h00)
    table_ref[...] = entry(table, 1, 0, h10)
    dots = [inner(b0, w1), inner(b1, w1), inner(w1, w1)]
    store_all(make_block(k2, dots, basis_ref[...], reach2_ref[...]), block_ref)


def fourth_kernel(
    total,
    b0_ref,
    k1_ref,
    b1_ref,
    k2_ref,
    table_in_ref,
    got_ref,
    pick_ref,
    near_ref,
    top_down_ref,
    coupling_ref,
    basis_ref,
    dots_ref,
    b2_ref,
    w2_ref,
    table_ref,
):
    k2 = k2_ref[...]
    image, dots = multiply(
        lambda: own_part(k2, near_ref),
        got_ref,
        pick_ref,
        near_ref,
        top_down_ref,
        coupling_ref,
        basis_ref,
    )
    b0, k1, b1 = b0_ref[...], k1_ref[...], b1_ref[...]
    h01 = dots[0] * (1.0 / total)
    h11 = dots[1] * (1.0 / total)
    h21, inv = norm_of(dots[2] * (1.0 / total), [h01, h11])
    shift = 0.5 - h11
    b2 = (shift * b1 + k2 - h01 * b0) * inv
    k3 = (shift * k2 + image - h01 * k1) * inv
    w2 = 0.5 * b2 + k3
    b2_ref[...] = b2
    w2_ref[...] = w2
    table = entry(table_in_ref[...], 0, 1, h01)
    table = entry(table, 1, 1, h11)
    table_ref[...] = entry(table, 2, 1, h21)
    val = in_lanes([inner(b0, w2), inner(b1, w2), inner(b2, w2), inner(w2, w2)], 0, 32)
    dots_ref[...] = jnp.broadcast_to(val[:1, :].reshape(1, 1, 128), dots_ref.shape)


def last_kernel(
    total, b0_ref, b1_ref, b2_ref, w2_ref, table_ref, dots_ref, out_ref, hessen_ref
):
    leaves = out_ref.shape[1]
    sums = jnp.sum(dots_ref[...], axis=0) * (1.0 / total)
    dots = [sums[:, 32 * i : 32 * i + 1] for i in range(4)]
    b0, b1, b2 = b0_ref[:leaves, :], b1_ref[:leaves, :], b2_ref[:leaves, :]
    scale, inv = norm_of(dots[3], dots[:3])
    update = w2_ref[:leaves, :] - dots[0] * b0 - dots[1] * b1 - dots[2] * b2
    out_ref[0] = b0
    out_ref[1] = b1
    out_ref[2] = b2
    out_ref[3] = update * inv
    table = table_ref[...]
    for i in range(3):
        table = entry(table, i, 2, dots[i])
    table = entry(table, 3, 2, scale)
    hessen_ref[...] = table[:4, :3]


def shaped(shape, dtype=F32):
    return jax.ShapeDtypeStruct(shape, dtype)


def call(kernel, ins, outs, scratch=(), cost=None):
    return pl.pallas_call(
        kernel,
        in_specs=ins,
        out_specs=[VMEM] * len(outs),
        out_shape=outs,
        scratch_shapes=scratch,
        cost_estimate=cost,
        compiler_params=pltpu.CompilerParams(vmem_limit_bytes=16 * 1024 * 1024),
    )


def per_device(
    start_vec,
    near_blocks,
    near_ids,
    far_ids,
    leaf_basis,
    leaf_coupling,
    node_transfer,
    branch_transfer,
    top_ids,
    top_coupling,
):
    subs = lax.axis_size("sub")
    devices = lax.axis_size("leaf") * subs
    leaves, size = start_vec.shape
    rank = leaf_basis.shape[1]
    total = float(leaves * size * devices)
    blocks = shaped((devices, 3, leaves, size // 2), BF16)
    vec = shaped((ROWS, size))
    table = shaped((ROWS, 128))

    def exchange(out):
        return lax.all_to_all(out, ("sub", "leaf"), 0, 0, tiled=True)

    sources = (
        start_vec,
        leaf_basis,
        node_transfer,
        branch_transfer,
        top_coupling,
        near_ids.T,
        far_ids.T,
        top_ids,
    )
    out, reach2, start2, pick, top_down = call(
        lambda *refs: first_kernel(subs, *refs),
        [HBM] * len(sources),
        [
            blocks,
            shaped((2 * rank, leaves * rank), BF16),
            vec,
            shaped((8 * ROWS, devices * leaves), BF16),
            shaped((leaves * rank, top_coupling.shape[2]), BF16),
        ],
        [pltpu.VMEM(a.shape, a.dtype) for a in sources]
        + [pltpu.SemaphoreType.DMA((len(sources),))],
        pl.CostEstimate(flops=2000000000, bytes_accessed=20000000, transcendentals=0),
    )(*[pltpu.with_memory_space_constraint(a, pltpu.HBM) for a in sources])
    fixed = (pick, near_blocks, top_down, leaf_coupling, leaf_basis)
    out, b0, k1 = call(
        lambda *refs: second_kernel(total, *refs), [VMEM] * 8, [blocks, vec, vec]
    )(start2, exchange(out), *fixed, reach2)
    out, b1, k2, heads = call(
        lambda *refs: third_kernel(total, *refs), [VMEM] * 9, [blocks, vec, vec, table]
    )(b0, k1, exchange(out), *fixed, reach2)
    dots, b2, w2, heads = call(
        lambda *refs: fourth_kernel(total, *refs),
        [VMEM] * 11,
        [shaped((devices, 1, 128)), vec, vec, table],
    )(b0, k1, b1, k2, heads, exchange(out), *fixed)
    basis, hessen = call(
        lambda *refs: last_kernel(total, *refs),
        [VMEM] * 6,
        [shaped((4, leaves, size)), shaped((4, 3))],
    )(b0, b1, b2, w2, heads, exchange(dots))
    return basis, hessen


def solution(mesh):
    placed = (
        P(("leaf", "sub"), None),
        P(("leaf", "sub"), None, None, None),
        P(("leaf", "sub"), None),
        P(("leaf", "sub"), None),
        P(("leaf", "sub"), None, None),
        P(("leaf", "sub"), None, None),
        P(("leaf", "sub"), None, None),
        P(("leaf", "sub"), None, None),
        P("leaf", None),
        P("leaf", None, None),
    )
    return jax.shard_map(
        per_device,
        mesh=mesh,
        in_specs=placed,
        out_specs=(P(None, ("leaf", "sub"), None), P()),
        check_vma=False,
    )
```

```python
import jax
import jax.numpy as jnp
from jax import lax
from jax.experimental import pallas as pl
from jax.experimental.pallas import tpu as pltpu
from jax.sharding import PartitionSpec as P

F32 = jnp.float32
BF16 = jnp.bfloat16
ROWS = 8
VMEM = pl.BlockSpec(memory_space=pltpu.VMEM)


def dot_nt(a, b):
    return lax.dot_general(a, b, (((1,), (1,)), ((), ())), preferred_element_type=F32)


def dot_nn(a, b):
    return lax.dot_general(a, b, (((1,), (0,)), ((), ())), preferred_element_type=F32)


def dot_tn(a, b):
    return lax.dot_general(a, b, (((0,), (0,)), ((), ())), preferred_element_type=F32)


def iota(shape, dim):
    return lax.broadcasted_iota(jnp.int32, shape, dim)


def twice(rows):
    return jnp.concatenate([rows, rows], axis=0)


def by_leaf(parts):
    row = iota(parts[0].shape, 0) % len(parts)
    total = parts[-1]
    for leaf in range(len(parts) - 1):
        total = jnp.where(row == leaf, parts[leaf], total)
    return total


def in_lanes(values, first, width):
    group = iota((ROWS, 128), 1) // width - first // width
    out = jnp.zeros((ROWS, 128), F32)
    for index, value in enumerate(values):
        out = jnp.where(group == index, value, out)
    return out


def inner(a, b):
    prod = a * b
    prod = prod[:, :128] + prod[:, 128:]
    return 0.5 * jnp.sum(jnp.sum(prod, axis=0, keepdims=True), axis=1, keepdims=True)


def is_mine(shape, rank, leaves):
    return iota(shape, 1) // rank == iota(shape, 0) % leaves


def make_block(vec, dots, basis, reach2):
    leaves, rank, size = basis.shape
    coef = dot_nt(vec.astype(BF16), basis.reshape(leaves * rank, size))
    coef = jnp.where(is_mine(coef.shape, rank, leaves), coef, 0.0)
    term = 0.5 * jnp.sum(dot_nt(coef.astype(BF16), reach2), axis=0, keepdims=True)
    coef = coef[:, :128] + coef[:, 128:]
    coef = coef + pltpu.roll(coef, rank, 1)
    val = in_lanes(dots, rank, 16)
    rest = val - val.astype(BF16).astype(F32)
    last = rest - rest.astype(BF16).astype(F32)
    row, low = iota((ROWS, 128), 0), iota((ROWS, 128), 1) < rank
    third = jnp.where(row == 0, term, jnp.where(row == 1, val, jnp.where(row == 2, rest, last)))
    third = jnp.where(low, coef, third)
    return [part[:leaves, :].astype(BF16) for part in (vec[:, :128], vec[:, 128:], third)]


def store_all(block, out_ref):
    devices = out_ref.shape[0]

    def store(device):
        for part in range(3):
            out_ref[device, part] = block[part]

    if devices <= 32:
        for device in range(devices):
            store(device)
    else:
        pl.loop(0, devices)(store)


def early_kernel(table_ref):
    table_ref[...] = jnp.zeros(table_ref.shape, F32)


def first_kernel(
    subs,
    start_ref,
    basis_ref,
    node_ref,
    upper_ref,
    top_ref,
    near_ids_ref,
    far_ids_ref,
    top_ids_ref,
    table_ref,
    block_ref,
    reach2_ref,
    start2_ref,
    pick_ref,
    top_down_ref,
):
    set_picks(subs, near_ids_ref[...], far_ids_ref[...], top_ids_ref[...], pick_ref)
    reach = dot_nn(upper_ref[0], node_ref[0])
    reach2 = twice(reach).astype(BF16)
    reach2_ref[...] = reach2
    start = twice(start_ref[...])
    start2_ref[...] = start
    store_all(make_block(start, [inner(start, start)], basis_ref[...], reach2), block_ref)
    top_down_ref[...] = dot_tn(reach.astype(BF16), top_ref[0]).astype(BF16)


def own_part(vec, near_ref):
    vec_bf = vec.astype(BF16)
    return by_leaf([dot_nt(vec_bf, near_ref[l, 0]) for l in range(near_ref.shape[0])])


def set_picks(subs, near_ids, far_ids, top_ids, pick_ref):
    branch = lax.axis_index("leaf").astype(jnp.int32)
    leaves = near_ids.shape[1]
    width = pick_ref.shape[1]
    col = iota((ROWS, width), 1)
    lane4, row4 = iota((ROWS, leaves), 1), iota((ROWS, leaves), 0) % leaves

    def by_row(ids):
        kept = jnp.where(lane4 == row4, ids, 0).astype(F32)
        return jnp.sum(kept, axis=1, keepdims=True).astype(jnp.int32)

    branches = width // (subs * leaves)

    def column(at, index):
        return ((index // leaves) * branches + at) * leaves + index % leaves

    ids = by_row(near_ids)
    at = branch - 1 + ids // (subs * leaves)
    inside = (at >= 0) & (at < branches)
    groups = [col == jnp.where(inside, column(at, ids % (subs * leaves)), -1)]
    for s in range(2):
        groups.append(col == column(branch, by_row(far_ids[s : s + 1, :])))
    for s in range(4):
        at = (col // leaves) % branches
        groups.append((col % leaves == 0) & (at == top_ids[0:1, s : s + 1]))
    groups.append(col % leaves > 0)
    pick_ref[...] = jnp.concatenate([g.astype(F32) for g in groups], axis=0).astype(BF16)


def multiply(own, got_ref, pick_ref, near_ref, top_down_ref, coupling_ref, basis_ref):
    leaves, rank, size = basis_ref.shape
    got = [got_ref[:, part].reshape(-1, 128) for part in range(3)]
    pick = pick_ref[...]
    rest = dot_nn(pick[ROWS:], got[2])
    other = jnp.concatenate([dot_nn(pick[:ROWS], got[0]), dot_nn(pick[:ROWS], got[1])], axis=1)
    near_out = own()
    group = [rest[ROWS * g : ROWS * g + ROWS, :] for g in range(7)]
    low = iota((ROWS, 128), 1) < rank
    far_in = jnp.where(low, group[0], pltpu.roll(group[1], rank, 1)).astype(BF16)
    top_a = jnp.where(low, pltpu.roll(group[2], rank, 1), group[3]).astype(BF16)
    top_b = jnp.where(low, pltpu.roll(group[4], rank, 1), group[5]).astype(BF16)
    top_in = jnp.concatenate([top_a, top_b], axis=1)
    local = dot_nt(far_in, coupling_ref[...].reshape(leaves * rank, -1))
    local = local + dot_nt(top_in, top_down_ref[...])
    other = other.astype(BF16)
    near_out = near_out + by_leaf([dot_nt(other, near_ref[l, 1]) for l in range(leaves)])
    local = jnp.where(is_mine(local.shape, rank, leaves), local, 0.0).astype(BF16)
    far_out = dot_nn(local, basis_ref[...].reshape(leaves * rank, size))
    dots = [group[6][:, rank + 16 * i : rank + 16 * i + 1] for i in range(4)]
    return near_out + far_out, dots


def entry(table, i, j, value):
    row, lane = iota(table.shape, 0), iota(table.shape, 1)
    return jnp.where((row == i) & (lane == j), value, table)


def norm_of(square, heads):
    remain = square
    for head in heads:
        remain = remain - head * head
    remain = jnp.maximum(remain, 0.01 * square)
    return jnp.sqrt(remain), lax.rsqrt(remain)


def second_kernel(
    total,
    start2_ref,
    got_ref,
    pick_ref,
    near_ref,
    top_down_ref,
    coupling_ref,
    basis_ref,
    reach2_ref,
    block_ref,
    b0_ref,
    k1_ref,
):
    start = start2_ref[...]
    image, dots = multiply(
        lambda: own_part(start, near_ref), got_ref, pick_ref, near_ref, top_down_ref, coupling_ref, basis_ref
    )
    scale = lax.rsqrt(dots[0] * (1.0 / total) + 1e-06)
    b0 = scale * start
    k1 = scale * image
    w0 = 0.5 * b0 + k1
    b0_ref[...] = b0
    k1_ref[...] = k1
    dots = [inner(b0, w0), inner(w0, w0)]
    store_all(make_block(k1, dots, basis_ref[...], reach2_ref[...]), block_ref)


def third_kernel(
    total,
    b0_ref,
    k1_ref,
    table_in_ref,
    got_ref,
    pick_ref,
    near_ref,
    top_down_ref,
    coupling_ref,
    basis_ref,
    reach2_ref,
    block_ref,
    b1_ref,
    k2_ref,
    table_ref,
):
    k1 = k1_ref[...]
    image, dots = multiply(
        lambda: own_part(k1, near_ref),
        got_ref,
        pick_ref,
        near_ref,
        top_down_ref,
        coupling_ref,
        basis_ref,
    )
    b0 = b0_ref[...]
    h00 = dots[0] * (1.0 / total)
    h10, inv = norm_of(dots[1] * (1.0 / total), [h00])
    shift = 0.5 - h00
    b1 = (shift * b0 + k1) * inv
    k2 = (shift * k1 + image) * inv
    w1 = 0.5 * b1 + k2
    b1_ref[...] = b1
    k2_ref[...] = k2
    table = entry(table_in_ref[...], 0, 0, h00)
    table_ref[...] = entry(table, 1, 0, h10)
    dots = [inner(b0, w1), inner(b1, w1), inner(w1, w1)]
    store_all(make_block(k2, dots, basis_ref[...], reach2_ref[...]), block_ref)


def fourth_kernel(
    total,
    b0_ref,
    k1_ref,
    b1_ref,
    k2_ref,
    table_in_ref,
    got_ref,
    pick_ref,
    near_ref,
    top_down_ref,
    coupling_ref,
    basis_ref,
    dots_ref,
    b2_ref,
    w2_ref,
    table_ref,
):
    k2 = k2_ref[...]
    image, dots = multiply(
        lambda: own_part(k2, near_ref),
        got_ref,
        pick_ref,
        near_ref,
        top_down_ref,
        coupling_ref,
        basis_ref,
    )
    b0, k1, b1 = b0_ref[...], k1_ref[...], b1_ref[...]
    h01 = dots[0] * (1.0 / total)
    h11 = dots[1] * (1.0 / total)
    h21, inv = norm_of(dots[2] * (1.0 / total), [h01, h11])
    shift = 0.5 - h11
    b2 = (shift * b1 + k2 - h01 * b0) * inv
    k3 = (shift * k2 + image - h01 * k1) * inv
    w2 = 0.5 * b2 + k3
    b2_ref[...] = b2
    w2_ref[...] = w2
    table = entry(table_in_ref[...], 0, 1, h01)
    table = entry(table, 1, 1, h11)
    table_ref[...] = entry(table, 2, 1, h21)
    val = in_lanes([inner(b0, w2), inner(b1, w2), inner(b2, w2), inner(w2, w2)], 0, 32)
    dots_ref[...] = jnp.broadcast_to(val[:1, :].reshape(1, 1, 128), dots_ref.shape)


def last_kernel(
    total, b0_ref, b1_ref, b2_ref, w2_ref, table_ref, dots_ref, out_ref, hessen_ref
):
    leaves = out_ref.shape[1]
    sums = jnp.sum(dots_ref[:, 0, :], axis=0, keepdims=True) * (1.0 / total)
    dots = [sums[:, 32 * i : 32 * i + 1] for i in range(4)]
    b0, b1, b2 = b0_ref[:leaves, :], b1_ref[:leaves, :], b2_ref[:leaves, :]
    scale, inv = norm_of(dots[3], dots[:3])
    update = w2_ref[:leaves, :] - dots[0] * b0 - dots[1] * b1 - dots[2] * b2
    out_ref[0] = b0
    out_ref[1] = b1
    out_ref[2] = b2
    out_ref[3] = update * inv
    table = table_ref[...]
    for i in range(3):
        table = entry(table, i, 2, dots[i])
    table = entry(table, 3, 2, scale)
    hessen_ref[...] = table[:4, :3]


def shaped(shape, dtype=F32):
    return jax.ShapeDtypeStruct(shape, dtype)


def call(kernel, ins, outs, cost=None):
    return pl.pallas_call(
        kernel,
        in_specs=ins,
        out_specs=[VMEM] * len(outs),
        out_shape=outs,
        cost_estimate=cost,
        compiler_params=pltpu.CompilerParams(vmem_limit_bytes=16 * 1024 * 1024),
    )


def per_device(
    start_vec,
    near_blocks,
    near_ids,
    far_ids,
    leaf_basis,
    leaf_coupling,
    node_transfer,
    branch_transfer,
    top_ids,
    top_coupling,
):
    subs = lax.axis_size("sub")
    devices = lax.axis_size("leaf") * subs
    leaves, size = start_vec.shape
    rank = leaf_basis.shape[1]
    total = float(leaves * size * devices)
    blocks = shaped((devices, 3, leaves, size // 2), BF16)
    vec = shaped((ROWS, size))
    table = shaped((ROWS, 128))

    def exchange(out):
        return lax.all_to_all(out, ("sub", "leaf"), 0, 0, tiled=True)

    sources = (
        start_vec,
        leaf_basis,
        node_transfer,
        branch_transfer,
        top_coupling,
        near_ids.T,
        far_ids.T,
        top_ids,
    )
    (heads,) = call(
        early_kernel,
        [],
        [table],
        pl.CostEstimate(flops=5000000000, bytes_accessed=20000000, transcendentals=0),
    )()
    out, reach2, start2, pick, top_down = call(
        lambda *refs: first_kernel(subs, *refs),
        [VMEM] * (len(sources) + 1),
        [
            blocks,
            shaped((2 * rank, leaves * rank), BF16),
            vec,
            shaped((8 * ROWS, devices * leaves), BF16),
            shaped((leaves * rank, top_coupling.shape[2]), BF16),
        ],
        pl.CostEstimate(flops=2000000000, bytes_accessed=20000000, transcendentals=0),
    )(*sources, heads)
    fixed = (pick, near_blocks, top_down, leaf_coupling, leaf_basis)
    out, b0, k1 = call(
        lambda *refs: second_kernel(total, *refs), [VMEM] * 8, [blocks, vec, vec]
    )(start2, exchange(out), *fixed, reach2)
    out, b1, k2, heads = call(
        lambda *refs: third_kernel(total, *refs), [VMEM] * 10, [blocks, vec, vec, table]
    )(b0, k1, heads, exchange(out), *fixed, reach2)
    dots, b2, w2, heads = call(
        lambda *refs: fourth_kernel(total, *refs),
        [VMEM] * 11,
        [shaped((devices, 1, 128)), vec, vec, table],
    )(b0, k1, b1, k2, heads, exchange(out), *fixed)
    basis, hessen = call(
        lambda *refs: last_kernel(total, *refs),
        [VMEM] * 6,
        [shaped((4, leaves, size)), shaped((4, 3))],
    )(b0, b1, b2, w2, heads, exchange(dots))
    return basis, hessen


def solution(mesh):
    placed = (
        P(("leaf", "sub"), None),
        P(("leaf", "sub"), None, None, None),
        P(("leaf", "sub"), None),
        P(("leaf", "sub"), None),
        P(("leaf", "sub"), None, None),
        P(("leaf", "sub"), None, None),
        P(("leaf", "sub"), None, None),
        P(("leaf", "sub"), None, None),
        P("leaf", None),
        P("leaf", None, None),
    )
    return jax.shard_map(
        per_device,
        mesh=mesh,
        in_specs=placed,
        out_specs=(P(None, ("leaf", "sub"), None), P()),
        check_vma=False,
    )
```

```python
import jax
import jax.numpy as jnp
from jax import lax
from jax.experimental import pallas as pl
from jax.experimental.pallas import tpu as pltpu
from jax.sharding import PartitionSpec as P

F32 = jnp.float32
BF16 = jnp.bfloat16
ROWS = 8
VMEM = pl.BlockSpec(memory_space=pltpu.VMEM)


def dot_nt(a, b):
    return lax.dot_general(a, b, (((1,), (1,)), ((), ())), preferred_element_type=F32)


def dot_nn(a, b):
    return lax.dot_general(a, b, (((1,), (0,)), ((), ())), preferred_element_type=F32)


def dot_tn(a, b):
    return lax.dot_general(a, b, (((0,), (0,)), ((), ())), preferred_element_type=F32)


def iota(shape, dim):
    return lax.broadcasted_iota(jnp.int32, shape, dim)


def twice(rows):
    return jnp.concatenate([rows, rows], axis=0)


def by_leaf(parts):
    row = iota(parts[0].shape, 0) % len(parts)
    total = parts[-1]
    for leaf in range(len(parts) - 1):
        total = jnp.where(row == leaf, parts[leaf], total)
    return total


def in_lanes(values, first, width):
    group = iota((ROWS, 128), 1) // width - first // width
    out = jnp.zeros((ROWS, 128), F32)
    for index, value in enumerate(values):
        out = jnp.where(group == index, value, out)
    return out


def inner(a, b):
    prod = a * b
    prod = prod[:, :128] + prod[:, 128:]
    return 0.5 * jnp.sum(jnp.sum(prod, axis=0, keepdims=True), axis=1, keepdims=True)


def is_mine(shape, rank, leaves):
    return iota(shape, 1) // rank == iota(shape, 0) % leaves


def make_block(vec, dots, basis, reach2):
    leaves, rank, size = basis.shape
    coef = dot_nt(vec.astype(BF16), basis.reshape(leaves * rank, size))
    coef = jnp.where(is_mine(coef.shape, rank, leaves), coef, 0.0)
    term = 0.5 * jnp.sum(dot_nt(coef.astype(BF16), reach2), axis=0, keepdims=True)
    coef = coef[:, :128] + coef[:, 128:]
    coef = coef + pltpu.roll(coef, rank, 1)
    val = in_lanes(dots, rank, 16)
    rest = val - val.astype(BF16).astype(F32)
    last = rest - rest.astype(BF16).astype(F32)
    row, low = iota((ROWS, 128), 0), iota((ROWS, 128), 1) < rank
    third = jnp.where(row == 0, term, jnp.where(row == 1, val, jnp.where(row == 2, rest, last)))
    third = jnp.where(low, coef, third)
    return [part[:leaves, :].astype(BF16) for part in (vec[:, :128], vec[:, 128:], third)]


def store_all(block, out_ref):
    devices = out_ref.shape[0]

    def store(device):
        for part in range(3):
            out_ref[device, part] = block[part]

    if devices <= 32:
        for device in range(devices):
            store(device)
    else:
        pl.loop(0, devices)(store)


def early_kernel(table_ref):
    table_ref[...] = jnp.zeros(table_ref.shape, F32)


def first_kernel(
    subs,
    start_ref,
    basis_ref,
    node_ref,
    upper_ref,
    top_ref,
    near_ids_ref,
    far_ids_ref,
    top_ids_ref,
    table_ref,
    block_ref,
    reach2_ref,
    start2_ref,
    pick_ref,
    top_down_ref,
    near_pick_ref,
    far_pick_ref,
    top_pick_ref,
):
    set_picks(
        subs,
        near_ids_ref[...],
        far_ids_ref[...],
        top_ids_ref[...],
        pick_ref,
        near_pick_ref,
        far_pick_ref,
        top_pick_ref,
    )
    reach = dot_nn(upper_ref[0], node_ref[0])
    reach2 = twice(reach).astype(BF16)
    reach2_ref[...] = reach2
    start = twice(start_ref[...])
    start2_ref[...] = start
    store_all(make_block(start, [inner(start, start)], basis_ref[...], reach2), block_ref)
    top_down_ref[...] = dot_tn(reach.astype(BF16), top_ref[0]).astype(BF16)


def own_part(vec, near_ref):
    vec_bf = vec.astype(BF16)
    return by_leaf([dot_nt(vec_bf, near_ref[l, 0]) for l in range(near_ref.shape[0])])


def set_picks(
    subs, near_ids, far_ids, top_ids, pick_ref, near_pick_ref, far_pick_ref, top_pick_ref
):
    branch = lax.axis_index("leaf").astype(jnp.int32)
    leaves = near_ids.shape[1]
    width = pick_ref.shape[1]
    col = iota((ROWS, width), 1)
    lane4, row4 = iota((ROWS, leaves), 1), iota((ROWS, leaves), 0) % leaves

    def by_row(ids):
        kept = jnp.where(lane4 == row4, ids, 0).astype(F32)
        return jnp.sum(kept, axis=1, keepdims=True).astype(jnp.int32)

    branches = top_pick_ref.shape[1]

    def column(at, index):
        return ((index // leaves) * branches + at) * leaves + index % leaves

    ids = by_row(near_ids)
    at = branch - 1 + ids // (subs * leaves)
    inside = (at >= 0) & (at < branches)
    groups = [col == jnp.where(inside, column(at, ids % (subs * leaves)), -1)]
    for s in range(2):
        groups.append(col == column(branch, by_row(far_ids[s : s + 1, :])))
    for s in range(4):
        at = (col // leaves) % branches
        groups.append((col % leaves == 0) & (at == top_ids[0:1, s : s + 1]))
    groups.append(col % leaves > 0)
    if pick_ref.shape[0] > ROWS:
        pick_ref[...] = jnp.concatenate([g.astype(F32) for g in groups], axis=0).astype(BF16)
    else:
        pick_ref[...] = jnp.zeros(pick_ref.shape, BF16)
    row = iota(near_pick_ref.shape[1:], 0)
    own_branch = branch * subs * leaves - subs * leaves
    outside = (row + own_branch < 0) | (row + own_branch >= branches * subs * leaves)
    for l in range(leaves):
        near_pick_ref[l] = (jnp.where(outside, -1, row) == near_ids[0:1, l : l + 1]).astype(F32)
    row = iota(far_pick_ref.shape[1:], 0)
    for s in range(2):
        for l in range(leaves):
            far_pick_ref[s * leaves + l] = (row == far_ids[s : s + 1, l : l + 1]).astype(F32)
    row = iota(top_pick_ref.shape[1:], 0)
    for s in range(4):
        top_pick_ref[s] = (row == top_ids[0:1, s : s + 1]).astype(F32)


def gather_rows(got_ref, near_pick_ref, far_pick_ref, top_pick_ref):
    branches = top_pick_ref.shape[1]
    leaves = got_ref.shape[2]
    subs = got_ref.shape[0] // branches
    branch = lax.axis_index("leaf").astype(jnp.int32)
    near_by = [got_ref[sub * branches + branch, 2].astype(F32) for sub in range(subs)]
    near_by = jnp.concatenate(near_by, axis=0)

    def chosen(masks, rows):
        return by_leaf(
            [
                jnp.broadcast_to(jnp.sum(mask * rows, axis=0, keepdims=True), (ROWS, 128))
                for mask in masks
            ]
        )

    group = [
        chosen([far_pick_ref[s * leaves + l] for l in range(leaves)], near_by) for s in range(2)
    ]
    about = [jnp.maximum(branch - 1, 0), branch, jnp.minimum(branch + 1, branches - 1)]
    halves = []
    for part in range(2):
        rows = [
            got_ref[sub * branches + at, part].astype(F32) for at in about for sub in range(subs)
        ]
        halves.append(
            chosen([near_pick_ref[l] for l in range(leaves)], jnp.concatenate(rows, axis=0))
        )
    other = jnp.concatenate(halves, axis=1)
    sums = [
        sum(got_ref[sub * branches + at, 2].astype(F32) for sub in range(subs))
        for at in range(branches)
    ]
    for s in range(4):
        row = sum(top_pick_ref[s, at : at + 1, :] * sums[at][:1, :] for at in range(branches))
        group.append(jnp.broadcast_to(row, (ROWS, 128)))
    total = sum(sums)
    group.append(total[1:2, :] + total[2:3, :] + total[3:4, :])
    return other, group


def multiply(
    own,
    got_ref,
    pick_ref,
    near_pick_ref,
    far_pick_ref,
    top_pick_ref,
    near_ref,
    top_down_ref,
    coupling_ref,
    basis_ref,
):
    leaves, rank, size = basis_ref.shape
    if pick_ref.shape[0] == ROWS:
        other, group = gather_rows(got_ref, near_pick_ref, far_pick_ref, top_pick_ref)
    else:
        got = [got_ref[:, part].reshape(-1, 128) for part in range(3)]
        pick = pick_ref[...]
        rest = dot_nn(pick[ROWS:], got[2])
        other = jnp.concatenate([dot_nn(pick[:ROWS], half) for half in got[:2]], axis=1)
        group = [rest[ROWS * g : ROWS * g + ROWS, :] for g in range(7)]
    near_out = own()
    low = iota((ROWS, 128), 1) < rank
    far_in = jnp.where(low, group[0], pltpu.roll(group[1], rank, 1)).astype(BF16)
    top_a = jnp.where(low, pltpu.roll(group[2], rank, 1), group[3]).astype(BF16)
    top_b = jnp.where(low, pltpu.roll(group[4], rank, 1), group[5]).astype(BF16)
    top_in = jnp.concatenate([top_a, top_b], axis=1)
    local = dot_nt(far_in, coupling_ref[...].reshape(leaves * rank, -1))
    local = local + dot_nt(top_in, top_down_ref[...])
    other = other.astype(BF16)
    near_out = near_out + by_leaf([dot_nt(other, near_ref[l, 1]) for l in range(leaves)])
    local = jnp.where(is_mine(local.shape, rank, leaves), local, 0.0).astype(BF16)
    far_out = dot_nn(local, basis_ref[...].reshape(leaves * rank, size))
    dots = [group[6][:, rank + 16 * i : rank + 16 * i + 1] for i in range(4)]
    return near_out + far_out, dots


def entry(table, i, j, value):
    row, lane = iota(table.shape, 0), iota(table.shape, 1)
    return jnp.where((row == i) & (lane == j), value, table)


def norm_of(square, heads):
    remain = square
    for head in heads:
        remain = remain - head * head
    remain = jnp.maximum(remain, 0.01 * square)
    return jnp.sqrt(remain), lax.rsqrt(remain)


def second_kernel(
    total,
    start2_ref,
    got_ref,
    pick_ref,
    near_pick_ref,
    far_pick_ref,
    top_pick_ref,
    near_ref,
    top_down_ref,
    coupling_ref,
    basis_ref,
    reach2_ref,
    block_ref,
    b0_ref,
    k1_ref,
):
    start = start2_ref[...]
    image, dots = multiply(
        lambda: own_part(start, near_ref),
        got_ref,
        pick_ref,
        near_pick_ref,
        far_pick_ref,
        top_pick_ref,
        near_ref,
        top_down_ref,
        coupling_ref,
        basis_ref,
    )
    scale = lax.rsqrt(dots[0] * (1.0 / total) + 1e-06)
    b0 = scale * start
    k1 = scale * image
    w0 = 0.5 * b0 + k1
    b0_ref[...] = b0
    k1_ref[...] = k1
    dots = [inner(b0, w0), inner(w0, w0)]
    store_all(make_block(k1, dots, basis_ref[...], reach2_ref[...]), block_ref)


def third_kernel(
    total,
    b0_ref,
    k1_ref,
    table_in_ref,
    got_ref,
    pick_ref,
    near_pick_ref,
    far_pick_ref,
    top_pick_ref,
    near_ref,
    top_down_ref,
    coupling_ref,
    basis_ref,
    reach2_ref,
    block_ref,
    b1_ref,
    k2_ref,
    table_ref,
):
    k1 = k1_ref[...]
    image, dots = multiply(
        lambda: own_part(k1, near_ref),
        got_ref,
        pick_ref,
        near_pick_ref,
        far_pick_ref,
        top_pick_ref,
        near_ref,
        top_down_ref,
        coupling_ref,
        basis_ref,
    )
    b0 = b0_ref[...]
    h00 = dots[0] * (1.0 / total)
    h10, inv = norm_of(dots[1] * (1.0 / total), [h00])
    shift = 0.5 - h00
    b1 = (shift * b0 + k1) * inv
    k2 = (shift * k1 + image) * inv
    w1 = 0.5 * b1 + k2
    b1_ref[...] = b1
    k2_ref[...] = k2
    table = entry(table_in_ref[...], 0, 0, h00)
    table_ref[...] = entry(table, 1, 0, h10)
    dots = [inner(b0, w1), inner(b1, w1), inner(w1, w1)]
    store_all(make_block(k2, dots, basis_ref[...], reach2_ref[...]), block_ref)


def fourth_kernel(
    total,
    b0_ref,
    k1_ref,
    b1_ref,
    k2_ref,
    table_in_ref,
    got_ref,
    pick_ref,
    near_pick_ref,
    far_pick_ref,
    top_pick_ref,
    near_ref,
    top_down_ref,
    coupling_ref,
    basis_ref,
    dots_ref,
    b2_ref,
    w2_ref,
    table_ref,
):
    k2 = k2_ref[...]
    image, dots = multiply(
        lambda: own_part(k2, near_ref),
        got_ref,
        pick_ref,
        near_pick_ref,
        far_pick_ref,
        top_pick_ref,
        near_ref,
        top_down_ref,
        coupling_ref,
        basis_ref,
    )
    b0, k1, b1 = b0_ref[...], k1_ref[...], b1_ref[...]
    h01 = dots[0] * (1.0 / total)
    h11 = dots[1] * (1.0 / total)
    h21, inv = norm_of(dots[2] * (1.0 / total), [h01, h11])
    shift = 0.5 - h11
    b2 = (shift * b1 + k2 - h01 * b0) * inv
    k3 = (shift * k2 + image - h01 * k1) * inv
    w2 = 0.5 * b2 + k3
    b2_ref[...] = b2
    w2_ref[...] = w2
    table = entry(table_in_ref[...], 0, 1, h01)
    table = entry(table, 1, 1, h11)
    table_ref[...] = entry(table, 2, 1, h21)
    val = in_lanes([inner(b0, w2), inner(b1, w2), inner(b2, w2), inner(w2, w2)], 0, 32)
    dots_ref[...] = jnp.broadcast_to(val[:1, :].reshape(1, 1, 128), dots_ref.shape)


def last_kernel(
    total, b0_ref, b1_ref, b2_ref, w2_ref, table_ref, dots_ref, out_ref, hessen_ref
):
    leaves = out_ref.shape[1]
    sums = jnp.sum(dots_ref[:, 0, :], axis=0, keepdims=True) * (1.0 / total)
    dots = [sums[:, 32 * i : 32 * i + 1] for i in range(4)]
    b0, b1, b2 = b0_ref[:leaves, :], b1_ref[:leaves, :], b2_ref[:leaves, :]
    scale, inv = norm_of(dots[3], dots[:3])
    update = w2_ref[:leaves, :] - dots[0] * b0 - dots[1] * b1 - dots[2] * b2
    out_ref[0] = b0
    out_ref[1] = b1
    out_ref[2] = b2
    out_ref[3] = update * inv
    table = table_ref[...]
    for i in range(3):
        table = entry(table, i, 2, dots[i])
    table = entry(table, 3, 2, scale)
    hessen_ref[...] = table[:4, :3]


def shaped(shape, dtype=F32):
    return jax.ShapeDtypeStruct(shape, dtype)


def call(kernel, ins, outs, cost=None):
    return pl.pallas_call(
        kernel,
        in_specs=ins,
        out_specs=[VMEM] * len(outs),
        out_shape=outs,
        cost_estimate=cost,
        compiler_params=pltpu.CompilerParams(vmem_limit_bytes=16 * 1024 * 1024),
    )


def per_device(
    start_vec,
    near_blocks,
    near_ids,
    far_ids,
    leaf_basis,
    leaf_coupling,
    node_transfer,
    branch_transfer,
    top_ids,
    top_coupling,
):
    subs = lax.axis_size("sub")
    devices = lax.axis_size("leaf") * subs
    leaves, size = start_vec.shape
    rank = leaf_basis.shape[1]
    total = float(leaves * size * devices)
    blocks = shaped((devices, 3, leaves, size // 2), BF16)
    vec = shaped((ROWS, size))
    table = shaped((ROWS, 128))

    def exchange(out):
        return lax.all_to_all(out, ("sub", "leaf"), 0, 0, tiled=True)

    sources = (
        start_vec,
        leaf_basis,
        node_transfer,
        branch_transfer,
        top_coupling,
        near_ids.T,
        far_ids.T,
        top_ids,
    )
    (heads,) = call(
        early_kernel,
        [],
        [table],
        pl.CostEstimate(flops=5000000000, bytes_accessed=20000000, transcendentals=0),
    )()
    picks = ROWS if devices <= 64 else 8 * ROWS
    out, reach2, start2, pick, top_down, near_pick, far_pick, top_pick = call(
        lambda *refs: first_kernel(subs, *refs),
        [VMEM] * (len(sources) + 1),
        [
            blocks,
            shaped((2 * rank, leaves * rank), BF16),
            vec,
            shaped((picks, devices * leaves), BF16),
            shaped((leaves * rank, top_coupling.shape[2]), BF16),
            shaped((leaves, 3 * subs * leaves, 128)),
            shaped((2 * leaves, subs * leaves, 128)),
            shaped((4, devices // subs, 128)),
        ],
        pl.CostEstimate(flops=2000000000, bytes_accessed=20000000, transcendentals=0),
    )(*sources, heads)
    fixed = (pick, near_pick, far_pick, top_pick, near_blocks, top_down, leaf_coupling, leaf_basis)
    out, b0, k1 = call(
        lambda *refs: second_kernel(total, *refs), [VMEM] * 11, [blocks, vec, vec]
    )(start2, exchange(out), *fixed, reach2)
    out, b1, k2, heads = call(
        lambda *refs: third_kernel(total, *refs), [VMEM] * 13, [blocks, vec, vec, table]
    )(b0, k1, heads, exchange(out), *fixed, reach2)
    dots, b2, w2, heads = call(
        lambda *refs: fourth_kernel(total, *refs),
        [VMEM] * 14,
        [shaped((devices, 1, 128)), vec, vec, table],
    )(b0, k1, b1, k2, heads, exchange(out), *fixed)
    basis, hessen = call(
        lambda *refs: last_kernel(total, *refs),
        [VMEM] * 6,
        [shaped((4, leaves, size)), shaped((4, 3))],
    )(b0, b1, b2, w2, heads, exchange(dots))
    return basis, hessen


def solution(mesh):
    placed = (
        P(("leaf", "sub"), None),
        P(("leaf", "sub"), None, None, None),
        P(("leaf", "sub"), None),
        P(("leaf", "sub"), None),
        P(("leaf", "sub"), None, None),
        P(("leaf", "sub"), None, None),
        P(("leaf", "sub"), None, None),
        P(("leaf", "sub"), None, None),
        P("leaf", None),
        P("leaf", None, None),
    )
    return jax.shard_map(
        per_device,
        mesh=mesh,
        in_specs=placed,
        out_specs=(P(None, ("leaf", "sub"), None), P()),
        check_vma=False,
    )
```

```python
import jax
import jax.numpy as jnp
from jax import lax
from jax.experimental import pallas as pl
from jax.experimental.pallas import tpu as pltpu
from jax.sharding import PartitionSpec as P

F32 = jnp.float32
BF16 = jnp.bfloat16
ROWS = 8
VMEM = pl.BlockSpec(memory_space=pltpu.VMEM)


def dot_nt(a, b):
    return lax.dot_general(a, b, (((1,), (1,)), ((), ())), preferred_element_type=F32)


def dot_nn(a, b):
    return lax.dot_general(a, b, (((1,), (0,)), ((), ())), preferred_element_type=F32)


def dot_tn(a, b):
    return lax.dot_general(a, b, (((0,), (0,)), ((), ())), preferred_element_type=F32)


def iota(shape, dim):
    return lax.broadcasted_iota(jnp.int32, shape, dim)


def twice(rows):
    return jnp.concatenate([rows, rows], axis=0)


def by_leaf(parts):
    row = iota(parts[0].shape, 0) % len(parts)
    total = parts[-1]
    for leaf in range(len(parts) - 1):
        total = jnp.where(row == leaf, parts[leaf], total)
    return total


def in_lanes(values, first, width):
    group = iota((ROWS, 128), 1) // width - first // width
    out = jnp.zeros((ROWS, 128), F32)
    for index, value in enumerate(values):
        out = jnp.where(group == index, value, out)
    return out


def inner(a, b):
    prod = a * b
    prod = prod[:, :128] + prod[:, 128:]
    return 0.5 * jnp.sum(jnp.sum(prod, axis=0, keepdims=True), axis=1, keepdims=True)


def is_mine(shape, rank, leaves):
    return iota(shape, 1) // rank == iota(shape, 0) % leaves


def make_block(vec, dots, basis, reach2):
    leaves, rank, size = basis.shape
    coef = dot_nt(vec.astype(BF16), basis.reshape(leaves * rank, size))
    coef = jnp.where(is_mine(coef.shape, rank, leaves), coef, 0.0)
    term = 0.5 * jnp.sum(dot_nt(coef.astype(BF16), reach2), axis=0, keepdims=True)
    coef = coef[:, :128] + coef[:, 128:]
    coef = coef + pltpu.roll(coef, rank, 1)
    val = in_lanes(dots, rank, 16)
    rest = val - val.astype(BF16).astype(F32)
    last = rest - rest.astype(BF16).astype(F32)
    row, low = iota((ROWS, 128), 0), iota((ROWS, 128), 1) < rank
    third = jnp.where(row == 0, term, jnp.where(row == 1, val, jnp.where(row == 2, rest, last)))
    third = jnp.where(low, coef, third)
    return [part[:leaves, :].astype(BF16) for part in (vec[:, :128], vec[:, 128:], third)]


def store_all(block, out_ref):
    devices = out_ref.shape[0]

    def store(device):
        for part in range(3):
            out_ref[device, part] = block[part]

    if devices <= 32:
        for device in range(devices):
            store(device)
    else:
        pl.loop(0, devices)(store)


def early_kernel(table_ref):
    table_ref[...] = jnp.zeros(table_ref.shape, F32)


def first_kernel(
    subs,
    start_ref,
    basis_ref,
    node_ref,
    upper_ref,
    near_ids_ref,
    far_ids_ref,
    top_ids_ref,
    table_ref,
    block_ref,
    reach2_ref,
    start2_ref,
    pick_ref,
    near_pick_ref,
    far_pick_ref,
    top_pick_ref,
):
    set_picks(
        subs,
        near_ids_ref[...],
        far_ids_ref[...],
        top_ids_ref[...],
        pick_ref,
        near_pick_ref,
        far_pick_ref,
        top_pick_ref,
    )
    reach = dot_nn(upper_ref[0], node_ref[0])
    reach2 = twice(reach).astype(BF16)
    reach2_ref[...] = reach2
    start = twice(start_ref[...])
    start2_ref[...] = start
    store_all(make_block(start, [inner(start, start)], basis_ref[...], reach2), block_ref)


def own_part(vec, near_ref):
    vec_bf = vec.astype(BF16)
    return by_leaf([dot_nt(vec_bf, near_ref[l, 0]) for l in range(near_ref.shape[0])])


def set_picks(
    subs, near_ids, far_ids, top_ids, pick_ref, near_pick_ref, far_pick_ref, top_pick_ref
):
    branch = lax.axis_index("leaf").astype(jnp.int32)
    leaves = near_ids.shape[1]
    width = pick_ref.shape[1]
    col = iota((ROWS, width), 1)
    lane4, row4 = iota((ROWS, leaves), 1), iota((ROWS, leaves), 0) % leaves

    def by_row(ids):
        kept = jnp.where(lane4 == row4, ids, 0).astype(F32)
        return jnp.sum(kept, axis=1, keepdims=True).astype(jnp.int32)

    branches = top_pick_ref.shape[1]

    def column(at, index):
        return ((index // leaves) * branches + at) * leaves + index % leaves

    ids = by_row(near_ids)
    at = branch - 1 + ids // (subs * leaves)
    inside = (at >= 0) & (at < branches)
    groups = [col == jnp.where(inside, column(at, ids % (subs * leaves)), -1)]
    for s in range(2):
        groups.append(col == column(branch, by_row(far_ids[s : s + 1, :])))
    for s in range(4):
        at = (col // leaves) % branches
        groups.append((col % leaves == 0) & (at == top_ids[0:1, s : s + 1]))
    groups.append(col % leaves > 0)
    if pick_ref.shape[0] > ROWS:
        pick_ref[...] = jnp.concatenate([g.astype(F32) for g in groups], axis=0).astype(BF16)
    else:
        pick_ref[...] = jnp.zeros(pick_ref.shape, BF16)
    row = iota(near_pick_ref.shape[1:], 0)
    own_branch = branch * subs * leaves - subs * leaves
    outside = (row + own_branch < 0) | (row + own_branch >= branches * subs * leaves)
    for l in range(leaves):
        near_pick_ref[l] = (jnp.where(outside, -1, row) == near_ids[0:1, l : l + 1]).astype(F32)
    row = iota(far_pick_ref.shape[1:], 0)
    for s in range(2):
        for l in range(leaves):
            far_pick_ref[s * leaves + l] = (row == far_ids[s : s + 1, l : l + 1]).astype(F32)
    row = iota(top_pick_ref.shape[1:], 0)
    for s in range(4):
        top_pick_ref[s] = (row == top_ids[0:1, s : s + 1]).astype(F32)


def gather_rows(got_ref, near_pick_ref, far_pick_ref, top_pick_ref):
    branches = top_pick_ref.shape[1]
    leaves = got_ref.shape[2]
    subs = got_ref.shape[0] // branches
    branch = lax.axis_index("leaf").astype(jnp.int32)
    near_by = [got_ref[sub * branches + branch, 2].astype(F32) for sub in range(subs)]
    near_by = jnp.concatenate(near_by, axis=0)

    def chosen(masks, rows):
        return by_leaf(
            [
                jnp.broadcast_to(jnp.sum(mask * rows, axis=0, keepdims=True), (ROWS, 128))
                for mask in masks
            ]
        )

    group = [
        chosen([far_pick_ref[s * leaves + l] for l in range(leaves)], near_by) for s in range(2)
    ]
    about = [jnp.maximum(branch - 1, 0), branch, jnp.minimum(branch + 1, branches - 1)]
    halves = []
    for part in range(2):
        rows = [
            got_ref[sub * branches + at, part].astype(F32) for at in about for sub in range(subs)
        ]
        halves.append(
            chosen([near_pick_ref[l] for l in range(leaves)], jnp.concatenate(rows, axis=0))
        )
    other = jnp.concatenate(halves, axis=1)
    sums = [
        sum(got_ref[sub * branches + at, 2].astype(F32) for sub in range(subs))
        for at in range(branches)
    ]
    for s in range(4):
        row = sum(top_pick_ref[s, at : at + 1, :] * sums[at][:1, :] for at in range(branches))
        group.append(jnp.broadcast_to(row, (ROWS, 128)))
    total = sum(sums)
    group.append(total[1:2, :] + total[2:3, :] + total[3:4, :])
    return other, group


def multiply(
    own,
    got_ref,
    pick_ref,
    near_pick_ref,
    far_pick_ref,
    top_pick_ref,
    near_ref,
    top_down_ref,
    coupling_ref,
    basis_ref,
):
    leaves, rank, size = basis_ref.shape
    if pick_ref.shape[0] == ROWS:
        other, group = gather_rows(got_ref, near_pick_ref, far_pick_ref, top_pick_ref)
    else:
        got = [got_ref[:, part].reshape(-1, 128) for part in range(3)]
        pick = pick_ref[...]
        rest = dot_nn(pick[ROWS:], got[2])
        other = jnp.concatenate([dot_nn(pick[:ROWS], half) for half in got[:2]], axis=1)
        group = [rest[ROWS * g : ROWS * g + ROWS, :] for g in range(7)]
    near_out = own()
    low = iota((ROWS, 128), 1) < rank
    far_in = jnp.where(low, group[0], pltpu.roll(group[1], rank, 1)).astype(BF16)
    top_a = jnp.where(low, pltpu.roll(group[2], rank, 1), group[3]).astype(BF16)
    top_b = jnp.where(low, pltpu.roll(group[4], rank, 1), group[5]).astype(BF16)
    top_in = jnp.concatenate([top_a, top_b], axis=1)
    local = dot_nt(far_in, coupling_ref[...].reshape(leaves * rank, -1))
    local = local + dot_nt(top_in, top_down_ref[...])
    other = other.astype(BF16)
    near_out = near_out + by_leaf([dot_nt(other, near_ref[l, 1]) for l in range(leaves)])
    local = jnp.where(is_mine(local.shape, rank, leaves), local, 0.0).astype(BF16)
    far_out = dot_nn(local, basis_ref[...].reshape(leaves * rank, size))
    dots = [group[6][:, rank + 16 * i : rank + 16 * i + 1] for i in range(4)]
    return near_out + far_out, dots


def entry(table, i, j, value):
    row, lane = iota(table.shape, 0), iota(table.shape, 1)
    return jnp.where((row == i) & (lane == j), value, table)


def norm_of(square, heads):
    remain = square
    for head in heads:
        remain = remain - head * head
    remain = jnp.maximum(remain, 0.01 * square)
    return jnp.sqrt(remain), lax.rsqrt(remain)


def second_kernel(
    total,
    start2_ref,
    got_ref,
    pick_ref,
    near_pick_ref,
    far_pick_ref,
    top_pick_ref,
    near_ref,
    top_ref,
    coupling_ref,
    basis_ref,
    reach2_ref,
    block_ref,
    b0_ref,
    k1_ref,
    top_down_ref,
):
    start = start2_ref[...]
    top_down_ref[...] = dot_tn(reach2_ref[: basis_ref.shape[1], :], top_ref[0]).astype(BF16)
    image, dots = multiply(
        lambda: own_part(start, near_ref),
        got_ref,
        pick_ref,
        near_pick_ref,
        far_pick_ref,
        top_pick_ref,
        near_ref,
        top_down_ref,
        coupling_ref,
        basis_ref,
    )
    scale = lax.rsqrt(dots[0] * (1.0 / total) + 1e-06)
    b0 = scale * start
    k1 = scale * image
    w0 = 0.5 * b0 + k1
    b0_ref[...] = b0
    k1_ref[...] = k1
    dots = [inner(b0, w0), inner(w0, w0)]
    store_all(make_block(k1, dots, basis_ref[...], reach2_ref[...]), block_ref)


def third_kernel(
    total,
    b0_ref,
    k1_ref,
    table_in_ref,
    got_ref,
    pick_ref,
    near_pick_ref,
    far_pick_ref,
    top_pick_ref,
    near_ref,
    top_down_ref,
    coupling_ref,
    basis_ref,
    reach2_ref,
    block_ref,
    b1_ref,
    k2_ref,
    table_ref,
):
    k1 = k1_ref[...]
    image, dots = multiply(
        lambda: own_part(k1, near_ref),
        got_ref,
        pick_ref,
        near_pick_ref,
        far_pick_ref,
        top_pick_ref,
        near_ref,
        top_down_ref,
        coupling_ref,
        basis_ref,
    )
    b0 = b0_ref[...]
    h00 = dots[0] * (1.0 / total)
    h10, inv = norm_of(dots[1] * (1.0 / total), [h00])
    shift = 0.5 - h00
    b1 = (shift * b0 + k1) * inv
    k2 = (shift * k1 + image) * inv
    w1 = 0.5 * b1 + k2
    b1_ref[...] = b1
    k2_ref[...] = k2
    table = entry(table_in_ref[...], 0, 0, h00)
    table_ref[...] = entry(table, 1, 0, h10)
    dots = [inner(b0, w1), inner(b1, w1), inner(w1, w1)]
    store_all(make_block(k2, dots, basis_ref[...], reach2_ref[...]), block_ref)


def fourth_kernel(
    total,
    b0_ref,
    k1_ref,
    b1_ref,
    k2_ref,
    table_in_ref,
    got_ref,
    pick_ref,
    near_pick_ref,
    far_pick_ref,
    top_pick_ref,
    near_ref,
    top_down_ref,
    coupling_ref,
    basis_ref,
    dots_ref,
    b2_ref,
    w2_ref,
    table_ref,
):
    k2 = k2_ref[...]
    image, dots = multiply(
        lambda: own_part(k2, near_ref),
        got_ref,
        pick_ref,
        near_pick_ref,
        far_pick_ref,
        top_pick_ref,
        near_ref,
        top_down_ref,
        coupling_ref,
        basis_ref,
    )
    b0, k1, b1 = b0_ref[...], k1_ref[...], b1_ref[...]
    h01 = dots[0] * (1.0 / total)
    h11 = dots[1] * (1.0 / total)
    h21, inv = norm_of(dots[2] * (1.0 / total), [h01, h11])
    shift = 0.5 - h11
    b2 = (shift * b1 + k2 - h01 * b0) * inv
    k3 = (shift * k2 + image - h01 * k1) * inv
    w2 = 0.5 * b2 + k3
    b2_ref[...] = b2
    w2_ref[...] = w2
    table = entry(table_in_ref[...], 0, 1, h01)
    table = entry(table, 1, 1, h11)
    table_ref[...] = entry(table, 2, 1, h21)
    val = in_lanes([inner(b0, w2), inner(b1, w2), inner(b2, w2), inner(w2, w2)], 0, 32)
    dots_ref[...] = jnp.broadcast_to(val[:1, :].reshape(1, 1, 128), dots_ref.shape)


def last_kernel(
    total, b0_ref, b1_ref, b2_ref, w2_ref, table_ref, dots_ref, out_ref, hessen_ref
):
    leaves = out_ref.shape[1]
    sums = jnp.sum(dots_ref[:, 0, :], axis=0, keepdims=True) * (1.0 / total)
    dots = [sums[:, 32 * i : 32 * i + 1] for i in range(4)]
    b0, b1, b2 = b0_ref[:leaves, :], b1_ref[:leaves, :], b2_ref[:leaves, :]
    scale, inv = norm_of(dots[3], dots[:3])
    update = w2_ref[:leaves, :] - dots[0] * b0 - dots[1] * b1 - dots[2] * b2
    out_ref[0] = b0
    out_ref[1] = b1
    out_ref[2] = b2
    out_ref[3] = update * inv
    table = table_ref[...]
    for i in range(3):
        table = entry(table, i, 2, dots[i])
    table = entry(table, 3, 2, scale)
    hessen_ref[...] = table[:4, :3]


def shaped(shape, dtype=F32):
    return jax.ShapeDtypeStruct(shape, dtype)


def call(kernel, ins, outs, cost=None):
    return pl.pallas_call(
        kernel,
        in_specs=ins,
        out_specs=[VMEM] * len(outs),
        out_shape=outs,
        cost_estimate=cost,
        compiler_params=pltpu.CompilerParams(vmem_limit_bytes=16 * 1024 * 1024),
    )


def per_device(
    start_vec,
    near_blocks,
    near_ids,
    far_ids,
    leaf_basis,
    leaf_coupling,
    node_transfer,
    branch_transfer,
    top_ids,
    top_coupling,
):
    subs = lax.axis_size("sub")
    devices = lax.axis_size("leaf") * subs
    leaves, size = start_vec.shape
    rank = leaf_basis.shape[1]
    total = float(leaves * size * devices)
    blocks = shaped((devices, 3, leaves, size // 2), BF16)
    vec = shaped((ROWS, size))
    table = shaped((ROWS, 128))

    def exchange(out):
        return lax.all_to_all(out, ("sub", "leaf"), 0, 0, tiled=True)

    sources = (
        start_vec,
        leaf_basis,
        node_transfer,
        branch_transfer,
        near_ids.T,
        far_ids.T,
        top_ids,
    )
    (heads,) = call(
        early_kernel,
        [],
        [table],
        pl.CostEstimate(flops=5000000000, bytes_accessed=20000000, transcendentals=0),
    )()
    picks = ROWS if devices <= 64 else 8 * ROWS
    out, reach2, start2, pick, near_pick, far_pick, top_pick = call(
        lambda *refs: first_kernel(subs, *refs),
        [VMEM] * (len(sources) + 1),
        [
            blocks,
            shaped((2 * rank, leaves * rank), BF16),
            vec,
            shaped((picks, devices * leaves), BF16),
            shaped((leaves, 3 * subs * leaves, 128)),
            shaped((2 * leaves, subs * leaves, 128)),
            shaped((4, devices // subs, 128)),
        ],
        pl.CostEstimate(flops=2000000000, bytes_accessed=20000000, transcendentals=0),
    )(*sources, heads)
    picked = (pick, near_pick, far_pick, top_pick, near_blocks)
    out, b0, k1, top_down = call(
        lambda *refs: second_kernel(total, *refs),
        [VMEM] * 11,
        [blocks, vec, vec, shaped((leaves * rank, top_coupling.shape[2]), BF16)],
    )(start2, exchange(out), *picked, top_coupling, leaf_coupling, leaf_basis, reach2)
    fixed = (*picked, top_down, leaf_coupling, leaf_basis)
    out, b1, k2, heads = call(
        lambda *refs: third_kernel(total, *refs), [VMEM] * 13, [blocks, vec, vec, table]
    )(b0, k1, heads, exchange(out), *fixed, reach2)
    dots, b2, w2, heads = call(
        lambda *refs: fourth_kernel(total, *refs),
        [VMEM] * 14,
        [shaped((devices, 1, 128)), vec, vec, table],
    )(b0, k1, b1, k2, heads, exchange(out), *fixed)
    basis, hessen = call(
        lambda *refs: last_kernel(total, *refs),
        [VMEM] * 6,
        [shaped((4, leaves, size)), shaped((4, 3))],
    )(b0, b1, b2, w2, heads, exchange(dots))
    return basis, hessen


def solution(mesh):
    placed = (
        P(("leaf", "sub"), None),
        P(("leaf", "sub"), None, None, None),
        P(("leaf", "sub"), None),
        P(("leaf", "sub"), None),
        P(("leaf", "sub"), None, None),
        P(("leaf", "sub"), None, None),
        P(("leaf", "sub"), None, None),
        P(("leaf", "sub"), None, None),
        P("leaf", None),
        P("leaf", None, None),
    )
    return jax.shard_map(
        per_device,
        mesh=mesh,
        in_specs=placed,
        out_specs=(P(None, ("leaf", "sub"), None), P()),
        check_vma=False,
    )
```

```python
import jax
import jax.numpy as jnp
from jax import lax
from jax.experimental import pallas as pl
from jax.experimental.pallas import tpu as pltpu
from jax.sharding import PartitionSpec as P

F32 = jnp.float32
BF16 = jnp.bfloat16
ROWS = 8
VMEM = pl.BlockSpec(memory_space=pltpu.VMEM)


def dot_nt(a, b):
    return lax.dot_general(a, b, (((1,), (1,)), ((), ())), preferred_element_type=F32)


def dot_nn(a, b):
    return lax.dot_general(a, b, (((1,), (0,)), ((), ())), preferred_element_type=F32)


def dot_tn(a, b):
    return lax.dot_general(a, b, (((0,), (0,)), ((), ())), preferred_element_type=F32)


def iota(shape, dim):
    return lax.broadcasted_iota(jnp.int32, shape, dim)


def twice(rows):
    return jnp.concatenate([rows, rows], axis=0)


def by_leaf(parts):
    row = iota(parts[0].shape, 0) % len(parts)
    total = parts[-1]
    for leaf in range(len(parts) - 1):
        total = jnp.where(row == leaf, parts[leaf], total)
    return total


def in_lanes(values, first, width):
    group = iota((ROWS, 128), 1) // width - first // width
    out = jnp.zeros((ROWS, 128), F32)
    for index, value in enumerate(values):
        out = jnp.where(group == index, value, out)
    return out


def inner(a, b):
    prod = a * b
    prod = prod[:, :128] + prod[:, 128:]
    return 0.5 * jnp.sum(jnp.sum(prod, axis=0, keepdims=True), axis=1, keepdims=True)


def is_mine(shape, rank, leaves):
    return iota(shape, 1) // rank == iota(shape, 0) % leaves


def make_block(vec, dots, basis, reach2):
    leaves, rank, size = basis.shape
    coef = dot_nt(vec.astype(BF16), basis.reshape(leaves * rank, size))
    coef = jnp.where(is_mine(coef.shape, rank, leaves), coef, 0.0)
    term = 0.5 * jnp.sum(dot_nt(coef.astype(BF16), reach2), axis=0, keepdims=True)
    coef = coef[:, :128] + coef[:, 128:]
    coef = coef + pltpu.roll(coef, rank, 1)
    val = in_lanes(dots, rank, 16)
    rest = val - val.astype(BF16).astype(F32)
    last = rest - rest.astype(BF16).astype(F32)
    row, low = iota((ROWS, 128), 0), iota((ROWS, 128), 1) < rank
    third = jnp.where(row == 0, term, jnp.where(row == 1, val, jnp.where(row == 2, rest, last)))
    third = jnp.where(low, coef, third)
    return [part[:leaves, :].astype(BF16) for part in (vec[:, :128], vec[:, 128:], third)]


def store_all(block, out_ref):
    devices = out_ref.shape[0]

    def store(device):
        for part in range(3):
            out_ref[device, part] = block[part]

    if devices <= 32:
        for device in range(devices):
            store(device)
    else:
        pl.loop(0, devices)(store)


def early_kernel(table_ref):
    table_ref[...] = jnp.zeros(table_ref.shape, F32)


def first_kernel(
    subs,
    start_ref,
    basis_ref,
    node_ref,
    upper_ref,
    top_ref,
    near_ids_ref,
    far_ids_ref,
    top_ids_ref,
    table_ref,
    block_ref,
    reach2_ref,
    start2_ref,
    pick_ref,
    top_down_ref,
    near_pick_ref,
    far_pick_ref,
    top_pick_ref,
):
    set_picks(
        subs,
        near_ids_ref[...],
        far_ids_ref[...],
        top_ids_ref[...],
        pick_ref,
        near_pick_ref,
        far_pick_ref,
        top_pick_ref,
    )
    reach = dot_nn(upper_ref[0], node_ref[0])
    reach2 = twice(reach).astype(BF16)
    reach2_ref[...] = reach2
    start = twice(start_ref[...])
    start2_ref[...] = start
    store_all(make_block(start, [inner(start, start)], basis_ref[...], reach2), block_ref)
    top_down_ref[...] = dot_tn(reach.astype(BF16), top_ref[0]).astype(BF16)


def own_part(vec, near_ref):
    vec_bf = vec.astype(BF16)
    return by_leaf([dot_nt(vec_bf, near_ref[l, 0]) for l in range(near_ref.shape[0])])


def set_picks(
    subs, near_ids, far_ids, top_ids, pick_ref, near_pick_ref, far_pick_ref, top_pick_ref
):
    branch = lax.axis_index("leaf").astype(jnp.int32)
    leaves = near_ids.shape[1]
    width = pick_ref.shape[1]
    col = iota((ROWS, width), 1)
    lane4, row4 = iota((ROWS, leaves), 1), iota((ROWS, leaves), 0) % leaves

    def by_row(ids):
        kept = jnp.where(lane4 == row4, ids, 0).astype(F32)
        return jnp.sum(kept, axis=1, keepdims=True).astype(jnp.int32)

    branches = top_pick_ref.shape[1]

    def column(at, index):
        return ((index // leaves) * branches + at) * leaves + index % leaves

    ids = by_row(near_ids)
    at = branch - 1 + ids // (subs * leaves)
    inside = (at >= 0) & (at < branches)
    groups = [col == jnp.where(inside, column(at, ids % (subs * leaves)), -1)]
    for s in range(2):
        groups.append(col == column(branch, by_row(far_ids[s : s + 1, :])))
    for s in range(4):
        at = (col // leaves) % branches
        groups.append((col % leaves == 0) & (at == top_ids[0:1, s : s + 1]))
    groups.append(col % leaves > 0)
    if pick_ref.shape[0] > ROWS:
        pick_ref[...] = jnp.concatenate([g.astype(F32) for g in groups], axis=0).astype(BF16)
    else:
        pick_ref[...] = jnp.zeros(pick_ref.shape, BF16)
    row = iota(near_pick_ref.shape[1:], 0)
    own_branch = branch * subs * leaves - subs * leaves
    outside = (row + own_branch < 0) | (row + own_branch >= branches * subs * leaves)
    for l in range(leaves):
        near_pick_ref[l] = (jnp.where(outside, -1, row) == near_ids[0:1, l : l + 1]).astype(F32)
    row = iota(far_pick_ref.shape[1:], 0)
    for s in range(2):
        for l in range(leaves):
            far_pick_ref[s * leaves + l] = (row == far_ids[s : s + 1, l : l + 1]).astype(F32)
    row = iota(top_pick_ref.shape[1:], 0)
    for s in range(4):
        top_pick_ref[s] = (row == top_ids[0:1, s : s + 1]).astype(F32)


def gather_rows(got_ref, near_pick_ref, far_pick_ref, top_pick_ref):
    branches = top_pick_ref.shape[1]
    leaves = got_ref.shape[2]
    subs = got_ref.shape[0] // branches
    branch = lax.axis_index("leaf").astype(jnp.int32)
    near_by = [got_ref[sub * branches + branch, 2].astype(F32) for sub in range(subs)]
    near_by = jnp.concatenate(near_by, axis=0)

    def chosen(masks, rows):
        return by_leaf(
            [
                jnp.broadcast_to(jnp.sum(mask * rows, axis=0, keepdims=True), (ROWS, 128))
                for mask in masks
            ]
        )

    group = [
        chosen([far_pick_ref[s * leaves + l] for l in range(leaves)], near_by) for s in range(2)
    ]
    about = [jnp.maximum(branch - 1, 0), branch, jnp.minimum(branch + 1, branches - 1)]
    halves = []
    for part in range(2):
        rows = [
            got_ref[sub * branches + at, part].astype(F32) for at in about for sub in range(subs)
        ]
        halves.append(
            chosen([near_pick_ref[l] for l in range(leaves)], jnp.concatenate(rows, axis=0))
        )
    other = jnp.concatenate(halves, axis=1)
    sums = [
        sum(got_ref[sub * branches + at, 2].astype(F32) for sub in range(subs))
        for at in range(branches)
    ]
    for s in range(4):
        row = sum(top_pick_ref[s, at : at + 1, :] * sums[at][:1, :] for at in range(branches))
        group.append(jnp.broadcast_to(row, (ROWS, 128)))
    total = sum(sums)
    group.append(total[1:2, :] + total[2:3, :] + total[3:4, :])
    return other, group


def multiply(
    own,
    got_ref,
    pick_ref,
    near_pick_ref,
    far_pick_ref,
    top_pick_ref,
    near_ref,
    top_down_ref,
    coupling_ref,
    basis_ref,
):
    leaves, rank, size = basis_ref.shape
    if pick_ref.shape[0] == ROWS:
        near_out = own()
        other, group = gather_rows(got_ref, near_pick_ref, far_pick_ref, top_pick_ref)
    else:
        got = [got_ref[:, part].reshape(-1, 128) for part in range(3)]
        pick = pick_ref[...]
        rest = dot_nn(pick[ROWS:], got[2])
        other = jnp.concatenate([dot_nn(pick[:ROWS], half) for half in got[:2]], axis=1)
        near_out = own()
        group = [rest[ROWS * g : ROWS * g + ROWS, :] for g in range(7)]
    low = iota((ROWS, 128), 1) < rank
    far_in = jnp.where(low, group[0], pltpu.roll(group[1], rank, 1)).astype(BF16)
    top_a = jnp.where(low, pltpu.roll(group[2], rank, 1), group[3]).astype(BF16)
    top_b = jnp.where(low, pltpu.roll(group[4], rank, 1), group[5]).astype(BF16)
    top_in = jnp.concatenate([top_a, top_b], axis=1)
    local = dot_nt(far_in, coupling_ref[...].reshape(leaves * rank, -1))
    local = local + dot_nt(top_in, top_down_ref[...])
    other = other.astype(BF16)
    near_out = near_out + by_leaf([dot_nt(other, near_ref[l, 1]) for l in range(leaves)])
    local = jnp.where(is_mine(local.shape, rank, leaves), local, 0.0).astype(BF16)
    far_out = dot_nn(local, basis_ref[...].reshape(leaves * rank, size))
    dots = [group[6][:, rank + 16 * i : rank + 16 * i + 1] for i in range(4)]
    return near_out + far_out, dots


def entry(table, i, j, value):
    row, lane = iota(table.shape, 0), iota(table.shape, 1)
    return jnp.where((row == i) & (lane == j), value, table)


def norm_of(square, heads):
    remain = square
    for head in heads:
        remain = remain - head * head
    remain = jnp.maximum(remain, 0.01 * square)
    return jnp.sqrt(remain), lax.rsqrt(remain)


def second_kernel(
    total,
    start2_ref,
    got_ref,
    pick_ref,
    near_pick_ref,
    far_pick_ref,
    top_pick_ref,
    near_ref,
    top_down_ref,
    coupling_ref,
    basis_ref,
    reach2_ref,
    block_ref,
    b0_ref,
    k1_ref,
):
    start = start2_ref[...]
    image, dots = multiply(
        lambda: own_part(start, near_ref),
        got_ref,
        pick_ref,
        near_pick_ref,
        far_pick_ref,
        top_pick_ref,
        near_ref,
        top_down_ref,
        coupling_ref,
        basis_ref,
    )
    scale = lax.rsqrt(dots[0] * (1.0 / total) + 1e-06)
    b0 = scale * start
    k1 = scale * image
    w0 = 0.5 * b0 + k1
    b0_ref[...] = b0
    k1_ref[...] = k1
    dots = [inner(b0, w0), inner(w0, w0)]
    store_all(make_block(k1, dots, basis_ref[...], reach2_ref[...]), block_ref)


def third_kernel(
    total,
    b0_ref,
    k1_ref,
    table_in_ref,
    got_ref,
    pick_ref,
    near_pick_ref,
    far_pick_ref,
    top_pick_ref,
    near_ref,
    top_down_ref,
    coupling_ref,
    basis_ref,
    reach2_ref,
    block_ref,
    b1_ref,
    k2_ref,
    table_ref,
):
    k1 = k1_ref[...]
    image, dots = multiply(
        lambda: own_part(k1, near_ref),
        got_ref,
        pick_ref,
        near_pick_ref,
        far_pick_ref,
        top_pick_ref,
        near_ref,
        top_down_ref,
        coupling_ref,
        basis_ref,
    )
    b0 = b0_ref[...]
    h00 = dots[0] * (1.0 / total)
    h10, inv = norm_of(dots[1] * (1.0 / total), [h00])
    shift = 0.5 - h00
    b1 = (shift * b0 + k1) * inv
    k2 = (shift * k1 + image) * inv
    w1 = 0.5 * b1 + k2
    b1_ref[...] = b1
    k2_ref[...] = k2
    table = entry(table_in_ref[...], 0, 0, h00)
    table_ref[...] = entry(table, 1, 0, h10)
    dots = [inner(b0, w1), inner(b1, w1), inner(w1, w1)]
    store_all(make_block(k2, dots, basis_ref[...], reach2_ref[...]), block_ref)


def fourth_kernel(
    total,
    b0_ref,
    k1_ref,
    b1_ref,
    k2_ref,
    table_in_ref,
    got_ref,
    pick_ref,
    near_pick_ref,
    far_pick_ref,
    top_pick_ref,
    near_ref,
    top_down_ref,
    coupling_ref,
    basis_ref,
    dots_ref,
    b2_ref,
    w2_ref,
    table_ref,
):
    k2 = k2_ref[...]
    image, dots = multiply(
        lambda: own_part(k2, near_ref),
        got_ref,
        pick_ref,
        near_pick_ref,
        far_pick_ref,
        top_pick_ref,
        near_ref,
        top_down_ref,
        coupling_ref,
        basis_ref,
    )
    b0, k1, b1 = b0_ref[...], k1_ref[...], b1_ref[...]
    h01 = dots[0] * (1.0 / total)
    h11 = dots[1] * (1.0 / total)
    h21, inv = norm_of(dots[2] * (1.0 / total), [h01, h11])
    shift = 0.5 - h11
    b2 = (shift * b1 + k2 - h01 * b0) * inv
    k3 = (shift * k2 + image - h01 * k1) * inv
    w2 = 0.5 * b2 + k3
    b2_ref[...] = b2
    w2_ref[...] = w2
    table = entry(table_in_ref[...], 0, 1, h01)
    table = entry(table, 1, 1, h11)
    table_ref[...] = entry(table, 2, 1, h21)
    val = in_lanes([inner(b0, w2), inner(b1, w2), inner(b2, w2), inner(w2, w2)], 0, 32)
    dots_ref[...] = jnp.broadcast_to(val[:1, :].reshape(1, 1, 128), dots_ref.shape)


def last_kernel(
    total, b0_ref, b1_ref, b2_ref, w2_ref, table_ref, dots_ref, out_ref, hessen_ref
):
    leaves = out_ref.shape[1]
    sums = jnp.sum(dots_ref[:, 0, :], axis=0, keepdims=True) * (1.0 / total)
    dots = [sums[:, 32 * i : 32 * i + 1] for i in range(4)]
    b0, b1, b2 = b0_ref[:leaves, :], b1_ref[:leaves, :], b2_ref[:leaves, :]
    scale, inv = norm_of(dots[3], dots[:3])
    update = w2_ref[:leaves, :] - dots[0] * b0 - dots[1] * b1 - dots[2] * b2
    out_ref[0] = b0
    out_ref[1] = b1
    out_ref[2] = b2
    out_ref[3] = update * inv
    table = table_ref[...]
    for i in range(3):
        table = entry(table, i, 2, dots[i])
    table = entry(table, 3, 2, scale)
    hessen_ref[...] = table[:4, :3]


def shaped(shape, dtype=F32):
    return jax.ShapeDtypeStruct(shape, dtype)


def call(kernel, ins, outs, cost=None):
    return pl.pallas_call(
        kernel,
        in_specs=ins,
        out_specs=[VMEM] * len(outs),
        out_shape=outs,
        cost_estimate=cost,
        compiler_params=pltpu.CompilerParams(vmem_limit_bytes=16 * 1024 * 1024),
    )


def per_device(
    start_vec,
    near_blocks,
    near_ids,
    far_ids,
    leaf_basis,
    leaf_coupling,
    node_transfer,
    branch_transfer,
    top_ids,
    top_coupling,
):
    subs = lax.axis_size("sub")
    devices = lax.axis_size("leaf") * subs
    leaves, size = start_vec.shape
    rank = leaf_basis.shape[1]
    total = float(leaves * size * devices)
    blocks = shaped((devices, 3, leaves, size // 2), BF16)
    vec = shaped((ROWS, size))
    table = shaped((ROWS, 128))

    def exchange(out):
        return lax.all_to_all(out, ("sub", "leaf"), 0, 0, tiled=True)

    sources = (
        start_vec,
        leaf_basis,
        node_transfer,
        branch_transfer,
        top_coupling,
        near_ids.T,
        far_ids.T,
        top_ids,
    )
    (heads,) = call(
        early_kernel,
        [],
        [table],
        pl.CostEstimate(flops=5000000000, bytes_accessed=20000000, transcendentals=0),
    )()
    picks = ROWS if devices <= 64 else 8 * ROWS
    out, reach2, start2, pick, top_down, near_pick, far_pick, top_pick = call(
        lambda *refs: first_kernel(subs, *refs),
        [VMEM] * (len(sources) + 1),
        [
            blocks,
            shaped((2 * rank, leaves * rank), BF16),
            vec,
            shaped((picks, devices * leaves), BF16),
            shaped((leaves * rank, top_coupling.shape[2]), BF16),
            shaped((leaves, 3 * subs * leaves, 128)),
            shaped((2 * leaves, subs * leaves, 128)),
            shaped((4, devices // subs, 128)),
        ],
        pl.CostEstimate(flops=2000000000, bytes_accessed=20000000, transcendentals=0),
    )(*sources, heads)
    fixed = (pick, near_pick, far_pick, top_pick, near_blocks, top_down, leaf_coupling, leaf_basis)
    out, b0, k1 = call(
        lambda *refs: second_kernel(total, *refs), [VMEM] * 11, [blocks, vec, vec]
    )(start2, exchange(out), *fixed, reach2)
    out, b1, k2, heads = call(
        lambda *refs: third_kernel(total, *refs), [VMEM] * 13, [blocks, vec, vec, table]
    )(b0, k1, heads, exchange(out), *fixed, reach2)
    dots, b2, w2, heads = call(
        lambda *refs: fourth_kernel(total, *refs),
        [VMEM] * 14,
        [shaped((devices, 1, 128)), vec, vec, table],
    )(b0, k1, b1, k2, heads, exchange(out), *fixed)
    basis, hessen = call(
        lambda *refs: last_kernel(total, *refs),
        [VMEM] * 6,
        [shaped((4, leaves, size)), shaped((4, 3))],
    )(b0, b1, b2, w2, heads, exchange(dots))
    return basis, hessen


def solution(mesh):
    placed = (
        P(("leaf", "sub"), None),
        P(("leaf", "sub"), None, None, None),
        P(("leaf", "sub"), None),
        P(("leaf", "sub"), None),
        P(("leaf", "sub"), None, None),
        P(("leaf", "sub"), None, None),
        P(("leaf", "sub"), None, None),
        P(("leaf", "sub"), None, None),
        P("leaf", None),
        P("leaf", None, None),
    )
    return jax.shard_map(
        per_device,
        mesh=mesh,
        in_specs=placed,
        out_specs=(P(None, ("leaf", "sub"), None), P()),
        check_vma=False,
    )
```
